128 devices in a mesh: ctx: 8 (over y, z_lo), shard: 16 (over x, z_hi, core).
Axes of the slice: x: 4, y: 4, z: 4 (z_hi: 2, z_lo: 2; z = z_hi * 2 + z_lo), core: 2. Of those that a mesh axis runs over, the one named last changes fastest.
Arguments:
- tokens: bfloat16 [16, 2048, 768], P('shard', 'ctx'), may hold values from -6 to 6
- lengths: int32 [16], P('shard'), may hold values from 1793 to 2048, as said below
- cotangent: bfloat16 [16, 2048, 768], P('shard', 'ctx'), may hold values from -6 to 6
- w_qkv: bfloat16 [768, 2304], P('shard'), may hold values from -0.3125 to 0.3125
- b_query: bfloat16 [768], P('shard'), may hold values from -1.1953125 to 1.1953125
- b_value: bfloat16 [768], P('shard'), may hold values from -1.1953125 to 1.1953125
- w_out: bfloat16 [768, 768], P('shard'), may hold values from -1.25 to 1.25
- b_out: bfloat16 [768], P('shard'), may hold values from -1.1953125 to 1.1953125
- gain_one: bfloat16 [768], P('shard'), may hold values from 0.5 to 1.5
- shift_one: bfloat16 [768], P('shard'), may hold values from -1.1953125 to 1.1953125
- w_up: bfloat16 [768, 3072], P('shard'), may hold values from -0.21875 to 0.21875
- b_up: bfloat16 [3072], P('shard'), may hold values from -1.1953125 to 1.1953125
- w_down: bfloat16 [3072, 768], P('shard'), may hold values from -0.109375 to 0.109375
- b_down: bfloat16 [768], P('shard'), may hold values from -1.1953125 to 1.1953125
- gain_two: bfloat16 [768], P('shard'), may hold values from 0.5 to 1.5
- shift_two: bfloat16 [768], P('shard'), may hold values from -1.1953125 to 1.1953125
Outputs:
- mixed: bfloat16 [16, 2048, 768], P('shard', 'ctx')
- grad_tokens: float32 [16, 2048, 768], P('shard', 'ctx')
- grad_w_qkv: float32 [768, 2304], P('shard')
- grad_b_query: float32 [768], P('shard')
- grad_b_value: float32 [768], P('shard')
- grad_w_out: float32 [768, 768], P('shard')
- grad_b_out: float32 [768], P('shard')
- grad_gain_one: float32 [768], P('shard')
- grad_shift_one: float32 [768], P('shard')
- grad_w_up: float32 [768, 3072], P('shard')
- grad_b_up: float32 [3072], P('shard')
- grad_w_down: float32 [3072, 768], P('shard')
- grad_b_down: float32 [768], P('shard')
- grad_gain_two: float32 [768], P('shard')
- grad_shift_two: float32 [768], P('shard')
The draws below stay inside these ranges and needn't reach their ends.
Inputs may be any that keep to these rules, and one draw needn't show every extreme that they name: lengths[s] is the number of valid tokens at the start of sequence s; one sequence, drawn from the seed, has all 2048.
All inputs are finite; a program needn't handle non-finite values.
Results may differ from the reference program's by a relative error of at most 0.025.
Values may be sent and summed in bfloat16 or wider, within the bound.
No kernel may reach another device: no remote copies, remote signals or barrier semaphores. Data moves between devices by JAX's collectives and lax.ppermute only.
A program may use at most 128 MiB of HBM per device.

```python
import jax
import jax.numpy as jnp
from jax import lax

D = 768
H = 12
HD = 64
FF = 3072
TOK_DEV = 256
LEN = 2048
SEQS = 16


def draw_lengths(key, part):
    key = jax.random.fold_in(key, 11)
    short_key, pick_key = jax.random.split(key)
    shortfall = jax.random.randint(short_key, (SEQS,), 0, TOK_DEV)
    chosen = jax.random.randint(pick_key, (), 0, SEQS)
    return jnp.where(jnp.arange(SEQS) == chosen, LEN, LEN - shortfall).astype(jnp.int32)


def steps_of(key, dims, cuts, least, top_value):
    def one(position, blocks):
        heights = jax.random.uniform(jax.random.fold_in(jax.random.fold_in(key, 6), position), (blocks,), jnp.float32, least / len(cuts), top_value / len(cuts))
        return jnp.repeat(jnp.exp(heights), dims[position] // blocks).reshape((-1,) + (1,) * (len(dims) - position - 1))

    level = one(*cuts[0])
    for cut in cuts[1:]:
        level = level * one(*cut)
    return level


def noise(own_key, shape, deviation, limit, shards=(), held_as=jnp.bfloat16):
    values = jax.random.normal(own_key, shape, jnp.float32) * deviation
    if len(shards) > 0:
        values = steps_of(own_key, shape, shards, -0.22, 0.18) * values
    return jnp.clip(values, min=-limit, max=limit).astype(held_as)


def setup_inputs(seed: int = 0) -> dict:
    seeds = jax.random.split(jax.random.key(seed), 17)
    tokens = noise(seeds[0], (SEQS, LEN, D), 1.0, 6.0, ((0, 16), (1, 8)))
    lengths = draw_lengths(jax.random.fold_in(seeds[16], 71), 0)
    cotangent = noise(seeds[2], (SEQS, LEN, D), 1.0, 6.0, ((0, 16), (1, 8)))
    w_qkv = noise(seeds[3], (D, 3 * D), (D // 2) ** -0.5, 0.3125, ((0, 16),))
    b_query = noise(seeds[4], (D,), 0.2, 1.1953125, ((0, 16),))
    b_value = noise(seeds[5], (D,), 0.2, 1.1953125, ((0, 16),))
    w_out = noise(seeds[6], (D, D), (D // 32) ** -0.5, 1.25, ((0, 16),))
    b_out = noise(seeds[7], (D,), 0.2, 1.1953125, ((0, 16),))
    gain_one = jnp.clip(1.0 + 0.1 * jax.random.normal(seeds[8], (D,), jnp.float32), 0.5, 1.5).astype(jnp.bfloat16)
    shift_one = noise(seeds[9], (D,), 0.2, 1.1953125, ((0, 16),))
    w_up = noise(seeds[10], (D, FF), D ** -0.5, 0.21875, ((0, 16),))
    b_up = noise(seeds[11], (FF,), 0.2, 1.1953125, ((0, 16),))
    w_down = noise(seeds[12], (FF, D), FF ** -0.5, 0.109375, ((0, 16),))
    b_down = noise(seeds[13], (D,), 0.2, 1.1953125, ((0, 16),))
    gain_two = jnp.clip(1.0 + 0.1 * jax.random.normal(seeds[14], (D,), jnp.float32), 0.5, 1.5).astype(jnp.bfloat16)
    shift_two = noise(seeds[15], (D,), 0.2, 1.1953125, ((0, 16),))
    return dict(tokens=tokens, lengths=lengths, cotangent=cotangent, w_qkv=w_qkv, b_query=b_query, b_value=b_value, w_out=w_out, b_out=b_out, gain_one=gain_one, shift_one=shift_one, w_up=w_up, b_up=b_up, w_down=w_down, b_down=b_down, gain_two=gain_two, shift_two=shift_two)


EPS = 1e-12
NEG = -1e+30
HIGH = lax.Precision.HIGHEST

@jax.custom_vjp
def low(v):
    return lax.optimization_barrier(v.astype(jnp.bfloat16)).astype(jnp.float32)

@jax.custom_vjp
def low_back(v):
    return v

def low_keep(v):
    return (low(v), None)

def low_pass(kept, grad):
    return (grad,)

def back_keep(v):
    return (v, None)

def back_low(kept, grad):
    return (low(grad),)
low.defvjp(low_keep, low_pass)
low_back.defvjp(back_keep, back_low)

def gelu_value(upward):
    return 0.5 * upward * (1.0 + lax.erf(upward * 0.7071067811865476))

def layer_norm(resid, gain, shift):
    mean = lax.optimization_barrier(jnp.mean(resid, axis=-1, keepdims=True))
    centered = resid - mean
    spread = lax.optimization_barrier(jnp.mean(centered * centered, axis=-1, keepdims=True))
    return centered * lax.rsqrt(spread + EPS) * gain + shift

def dense_prod(left, right):
    return jnp.dot(left, right, precision=HIGH)

def attend_rows(query_rows, key_heads, value_heads, key_live):
    scores = low_back(jnp.einsum('thd,shd->hts', query_rows, key_heads, precision=HIGH) * HD ** (-0.5))
    masked = jnp.where(key_live[None, None, :], scores, NEG)
    row_max = lax.optimization_barrier(jnp.max(masked, axis=-1, keepdims=True))
    row_total = lax.optimization_barrier(jnp.sum(jnp.where(key_live[None, None, :], jnp.exp(masked - row_max), 0.0), axis=-1, keepdims=True))
    log_total = row_max + jnp.log(row_total)
    soft_weights = jnp.where(key_live[None, None, :], jnp.exp(masked - log_total), 0.0)
    return jnp.einsum('hts,shd->thd', low(soft_weights), value_heads, precision=HIGH)

def sequence_forward(token_seq, length, params):
    w_qkv, b_query, b_value, w_out, b_out, gain_one, shift_one, w_up, b_up, w_down, b_down, gain_two, shift_two = params
    projected = low_back(dense_prod(token_seq, w_qkv))
    queries = low(projected[:, :D] + b_query)
    key_rows = low(projected[:, D:2 * D]).reshape(LEN, H, HD)
    value_rows = low(projected[:, 2 * D:] + b_value).reshape(LEN, H, HD)
    key_live = jnp.arange(LEN, dtype=jnp.int32) < length
    block_rows = min(512, LEN)
    query_blocks = queries.reshape(LEN // block_rows, block_rows, H, HD)
    attended = lax.map(jax.checkpoint(lambda rows_in: attend_rows(rows_in, key_rows, value_rows, key_live)), query_blocks)
    attended = low(low_back(attended.reshape(LEN, D)))
    resid_one = token_seq + low_back(dense_prod(attended, w_out)) + b_out
    hidden = layer_norm(resid_one, gain_one, shift_one)
    upward = low_back(dense_prod(low(hidden), w_up)) + b_up
    resid_two = hidden + low_back(dense_prod(low(gelu_value(upward)), w_down)) + b_down
    return layer_norm(resid_two, gain_two, shift_two)

def reference(tokens, lengths, cotangent, w_qkv, b_query, b_value, w_out, b_out, gain_one, shift_one, w_up, b_up, w_down, b_down, gain_two, shift_two):
    params = tuple((argument.astype(jnp.float32) for argument in (w_qkv, b_query, b_value, w_out, b_out, gain_one, shift_one, w_up, b_up, w_down, b_down, gain_two, shift_two)))

    def forward(token_rows, weights):
        return lax.map(jax.checkpoint(lambda seq_pair: sequence_forward(seq_pair[0], seq_pair[1], weights)), (token_rows, lengths))
    mixed, pullback = jax.vjp(forward, tokens.astype(jnp.float32), params)
    grad_tokens, grads = pullback(cotangent.astype(jnp.float32))
    return (mixed.astype(jnp.bfloat16), grad_tokens, grads[0], grads[1], grads[2], grads[3], grads[4], grads[5], grads[6], grads[7], grads[8], grads[9], grads[10], grads[11], grads[12])
```

```python
import jax
import jax.numpy as jnp
from jax import lax
from jax.experimental import pallas as pl
from jax.experimental.pallas import tpu as pltpu
from jax.sharding import PartitionSpec as P

H = 12
HD = 64
GROUP = 3
CTX = 8
SHARD = 16
AXES = ("ctx", "shard")
EPS = 1e-12
NEG = -1e30
SCALE = HD ** (-0.5)
BF = jnp.bfloat16
F32 = jnp.float32


def place(device):
    ctx, shard = divmod(device, SHARD)
    return [shard // 4, ctx // 2, (shard // 2) % 2, ctx % 2, shard % 2]


def device_at(x, y, z_hi, z_lo, core):
    return (y * 2 + z_lo) * SHARD + x * 4 + z_hi * 2 + core


def moved(value, x=0, y=0, z_hi=0, z_lo=0, core=0):
    pairs = []
    for source in range(CTX * SHARD):
        a, b, c, d, e = place(source)
        target = device_at((a + x) % 4, (b + y) % 4, (c + z_hi) % 2, (d + z_lo) % 2, (e + core) % 2)
        pairs.append((source, target))
    return lax.ppermute(value, AXES, pairs)


def groups_along(*axes):
    found = {}
    for device in range(CTX * SHARD):
        at = place(device)
        key = tuple(v for i, v in enumerate(at) if i not in axes)
        found.setdefault(key, []).append((tuple(at[i] for i in axes), device))
    return [[d for _, d in sorted(members)] for members in found.values()]


def exchanged(blocks, *axes):
    return lax.all_to_all(blocks, AXES, 0, 0, axis_index_groups=groups_along(*axes))


def gathered(block, *axes):
    count = len(groups_along(*axes)[0])
    return exchanged(jnp.broadcast_to(block[None], (count, *block.shape)), *axes)


def total(blocks, dim=0):
    return jnp.sum(blocks.astype(F32), axis=dim)


def pick(blocks, index, dim=0):
    return lax.dynamic_index_in_dim(blocks, index, dim, keepdims=False)


def with_rows(block, rows):
    at = lax.broadcasted_iota(jnp.int32, (16, block.shape[1]), 0)
    extra = jnp.zeros((16, block.shape[1]), F32)
    for place_, row in enumerate(rows):
        extra = jnp.where(at == place_, row, extra)
    rest = jnp.zeros((48, block.shape[1]), BF)
    return jnp.concatenate([block, extra.astype(BF), rest], axis=0)


def turned(block):
    return block.astype(F32).T.astype(BF)


def live_row(limit):
    tokens = lax.broadcasted_iota(jnp.int32, (1, 256), 1)
    return jnp.where(tokens < limit, 0.0, NEG)


def forward_kernel(limits, *refs):
    near, far = refs[0:4], refs[4:8]
    out_low, out_full, log_total = refs[8:12], refs[12], refs[13]
    key_scr, value_scr = refs[14], refs[15]
    ones = jnp.ones((1, 256), F32)
    for c in range(8):
        keys = near[c][1, 0] if c < 4 else far[c - 4][0, 0]
        values = near[c][2, 0] if c < 4 else far[c - 4][1, 0]
        key_scr[c] = turned(with_rows(keys, [live_row(limits[c])]))
        value_scr[c] = with_rows(values, [ones])[:80]
    for b in range(4):
        queries = with_rows((near[b][0, 0].astype(F32) * SCALE).astype(BF), [ones])
        scores = [
            jnp.dot(key_scr[c], queries, preferred_element_type=F32) for c in range(8)
        ]
        top = scores[0]
        for c in range(1, 8):
            top = jnp.maximum(top, scores[c])
        row_max = jnp.max(top, axis=0, keepdims=True)
        out = jnp.zeros((80, 256), F32)
        for c in range(8):
            weights = jnp.exp(scores[c] - row_max).astype(BF)
            out = out + jnp.dot(value_scr[c], weights, preferred_element_type=F32)
        row_total = out[64:65]
        attended = out[:64] / row_total
        out_low[b][0] = attended.astype(BF)
        out_full[0, b] = attended
        log_total[0, b : b + 1] = row_max + jnp.log(row_total)


def forward_attention(limits, near, far):
    head = lambda h: (0, h, 0, 0)
    return pl.pallas_call(
        forward_kernel,
        grid=(GROUP,),
        in_specs=[pl.BlockSpec(memory_space=pltpu.SMEM)]
        + [pl.BlockSpec((3, 1, HD, 256), head)] * 4
        + [pl.BlockSpec((2, 1, HD, 256), head)] * 4,
        out_specs=[pl.BlockSpec((1, HD, 256), lambda h: (h, 0, 0))] * 4
        + [
            pl.BlockSpec((1, 4, HD, 256), lambda h: (h, 0, 0, 0)),
            pl.BlockSpec((1, 4, 256), lambda h: (h, 0, 0)),
        ],
        out_shape=[jax.ShapeDtypeStruct((GROUP, HD, 256), BF)] * 4
        + [
            jax.ShapeDtypeStruct((GROUP, 4, HD, 256), F32),
            jax.ShapeDtypeStruct((GROUP, 4, 256), F32),
        ],
        scratch_shapes=[pltpu.VMEM((8, 256, 128), BF), pltpu.VMEM((8, 80, 256), BF)],
        compiler_params=pltpu.CompilerParams(vmem_limit_bytes=40 * 2**20),
        cost_estimate=pl.CostEstimate(
            flops=12 * 2048 * 256 * 512, bytes_accessed=6 * 2**20, transcendentals=12 * 2048 * 256
        ),
        name="attention_forward",
    )(limits, *near, *far)


def split_rows(row, count):
    parts = []
    for _ in range(count):
        part = row.astype(BF).astype(F32)
        parts.append(part)
        row = row - part
    return parts


def backward_kernel(limits, *refs):
    near, far, grads = refs[0:4], refs[4:8], refs[8:12]
    out_full, log_total = refs[12], refs[13]
    grad_near, grad_far = refs[14:18], refs[18:22]
    query_scr, query_turned, grad_scr, grad_turned = refs[22:26]
    ones = jnp.ones((1, 256), F32)
    for b in range(4):
        at = slice(256 * b, 256 * b + 256)
        log_rows = split_rows(-log_total[0, b : b + 1], 3)
        queries = with_rows((near[b][0, 0].astype(F32) * SCALE).astype(BF), [ones] + log_rows)
        query_scr[:, at] = queries
        query_turned[at, :] = turned(queries)
        delta = jnp.sum(grads[b][0].astype(F32) * out_full[0, b], axis=0, keepdims=True)
        grad = with_rows(grads[b][0], split_rows(-delta, 2))
        grad_scr[:, at] = grad
        grad_turned[at, :] = turned(grad)
    grad_queries = jnp.zeros((HD, 1024), F32)
    for c in range(8):
        keys = near[c][1, 0] if c < 4 else far[c - 4][0, 0]
        values = near[c][2, 0] if c < 4 else far[c - 4][1, 0]
        key_rows = turned(with_rows(keys, [live_row(limits[c]), ones, ones, ones]))
        value_rows = turned(with_rows(values, [ones, ones]))
        weights = jnp.exp(jnp.dot(key_rows, query_scr[...], preferred_element_type=F32))
        grad_soft = jnp.dot(value_rows, grad_scr[...], preferred_element_type=F32)
        grad_scores = (weights * grad_soft).astype(BF)
        grad_values = jnp.dot(weights.astype(BF), grad_turned[...], preferred_element_type=F32)
        grad_keys = jnp.dot(grad_scores, query_turned[...], preferred_element_type=F32)
        grad_queries = grad_queries + jnp.dot(keys, grad_scores, preferred_element_type=F32)
        to, first = (grad_near[c], 1) if c < 4 else (grad_far[c - 4], 0)
        to[first, 0] = grad_keys.T[:HD].astype(BF)
        to[first + 1, 0] = grad_values.T[:HD].astype(BF)
    for b in range(4):
        grad_near[b][0, 0] = (grad_queries[:, 256 * b : 256 * b + 256] * SCALE).astype(BF)


def backward_attention(limits, near, far, grads, out_full, log_total):
    head = lambda h: (0, h, 0, 0)
    near_spec = pl.BlockSpec((3, 1, HD, 256), head)
    far_spec = pl.BlockSpec((2, 1, HD, 256), head)
    return pl.pallas_call(
        backward_kernel,
        grid=(GROUP,),
        in_specs=[pl.BlockSpec(memory_space=pltpu.SMEM)]
        + [near_spec] * 4
        + [far_spec] * 4
        + [pl.BlockSpec((1, HD, 256), lambda h: (h, 0, 0))] * 4
        + [
            pl.BlockSpec((1, 4, HD, 256), lambda h: (h, 0, 0, 0)),
            pl.BlockSpec((1, 4, 256), lambda h: (h, 0, 0)),
        ],
        out_specs=[near_spec] * 4 + [far_spec] * 4,
        out_shape=[jax.ShapeDtypeStruct((3, GROUP, HD, 256), BF)] * 4
        + [jax.ShapeDtypeStruct((2, GROUP, HD, 256), BF)] * 4,
        scratch_shapes=[
            pltpu.VMEM((128, 1024), BF),
            pltpu.VMEM((1024, 128), BF),
            pltpu.VMEM((128, 1024), BF),
            pltpu.VMEM((1024, 128), BF),
        ],
        compiler_params=pltpu.CompilerParams(vmem_limit_bytes=40 * 2**20),
        cost_estimate=pl.CostEstimate(
            flops=12 * 2048 * 256 * 1280, bytes_accessed=12 * 2**20, transcendentals=12 * 2048 * 256
        ),
        name="attention_backward",
    )(limits, *near, *far, *grads, out_full, log_total)


def gelu_value(upward):
    return 0.5 * upward * (1.0 + lax.erf(upward * 0.7071067811865476))


def gelu_slope(upward):
    return (
        0.5 * (1.0 + lax.erf(upward * 0.7071067811865476))
        + upward * jnp.exp(-0.5 * upward * upward) * 0.3989422804014327
    )


def layer_norm(resid, gain, shift):
    mean = jnp.mean(resid, axis=-1, keepdims=True)
    centered = resid - mean
    spread = jnp.mean(centered * centered, axis=-1, keepdims=True)
    inverse = lax.rsqrt(spread + EPS)
    normed = centered * inverse
    return (normed * gain + shift, normed, inverse)


def norm_back(grad_out, normed, inverse, gain):
    grad_normed = grad_out * gain
    return inverse * (
        grad_normed
        - jnp.mean(grad_normed, axis=-1, keepdims=True)
        - normed * jnp.mean(grad_normed * normed, axis=-1, keepdims=True)
    )


def product(spec, left, right):
    return jnp.einsum(spec, left, right, preferred_element_type=F32)


def vector_rows(vectors):
    row = jnp.concatenate([v.astype(BF) for v in vectors], axis=-1)
    row = jnp.pad(row, [(0, 0)] * (row.ndim - 1) + [(0, 768 - row.shape[-1])])
    return jnp.pad(row[..., None, :], [(0, 0)] * (row.ndim - 1) + [(0, 15), (0, 0)])


def sum_over_all(blocks, x_first, place_now):
    x, y, z_hi, core = place_now
    rows = blocks.shape[1]
    pairs = blocks.reshape(8, 2, rows, 768)
    mine = pick(pairs, core, 1)
    other = moved(pick(pairs, 1 - core, 1), core=1)
    units = (mine.astype(F32) + other.astype(F32)).astype(BF)
    if x_first:
        units = units.reshape(4, 2, rows, 768)
        own = pick(units, x).astype(F32)
        for d in (1, 3, 2):
            own = own + moved(pick(units, (x + d) % 4), x=d).astype(F32)
        own = own.astype(BF)
        partial = pick(own, z_hi).astype(F32) + moved(pick(own, 1 - z_hi), z_hi=1, z_lo=1).astype(F32)
        quarters = partial.astype(BF).reshape(4, rows // 4, 768)
        mine = pick(quarters, y).astype(F32)
        for d in (1, 3, 2):
            mine = mine + moved(pick(quarters, (y + d) % 4), y=d).astype(F32)
    else:
        quarters = units.reshape(8, 4, rows // 4, 768).transpose(1, 0, 2, 3)
        units = total(exchanged(quarters, 1)).astype(BF)
        mine = total(exchanged(units, 0, 2))
    mine = mine.astype(BF)
    mine = (mine.astype(F32) + moved(mine, z_lo=1).astype(F32)).astype(BF)
    return gathered(mine, 1).reshape(rows, 768)


def local(
    tokens,
    lengths,
    cotangent,
    w_qkv,
    b_query,
    b_value,
    w_out,
    b_out,
    gain_one,
    shift_one,
    w_up,
    b_up,
    w_down,
    b_down,
    gain_two,
    shift_two,
):
    ctx, shard = lax.axis_index("ctx"), lax.axis_index("shard")
    y, z_lo = ctx // 2, ctx % 2
    x, z_hi, core = shard // 4, (shard // 2) % 2, shard % 2
    place_now = (x, y, z_hi, core)
    width = 768
    x_low = tokens[0]

    qkv_own = jnp.concatenate(
        [w_qkv[:, :width], w_qkv[:, width : 2 * width], w_qkv[:, 2 * width :], vector_rows([b_query, b_value])],
        axis=0,
    )
    rest_own = jnp.concatenate(
        [w_out]
        + [w_up[:, width * i : width * (i + 1)] for i in range(4)]
        + [w_down, vector_rows([b_out, gain_one, shift_one, b_down, gain_two, shift_two, b_up])],
        axis=0,
    )
    rest = lax.all_gather(rest_own, "shard", axis=0, tiled=True).reshape(SHARD, 448, width)

    other = moved(qkv_own, z_hi=1, z_lo=1)
    both = jnp.where(z_hi == 0, jnp.stack([qkv_own, other]), jnp.stack([other, qkv_own]))
    along_x = gathered(both, 0)
    other = moved(along_x, core=1)
    qkv_all = jnp.where(
        core == 0, jnp.stack([along_x, other], axis=2), jnp.stack([other, along_x], axis=2)
    ).reshape(SHARD, 160, width)
    w_parts = [qkv_all[:, 48 * i : 48 * i + 48].reshape(width, width) for i in range(3)]
    b_query = qkv_all[:, 144, 0:48].reshape(width).astype(F32)
    b_value = qkv_all[:, 144, 48:96].reshape(width).astype(F32)

    queries = (product("dk,td->kt", w_parts[0], x_low) + b_query[:, None]).astype(BF)
    keys = product("dk,td->kt", w_parts[1], x_low).astype(BF)
    values = (product("dk,td->kt", w_parts[2], x_low) + b_value[:, None]).astype(BF)
    stacked = jnp.stack([queries, keys, values]).reshape(3, 4, GROUP, HD, 256)

    near, far = [pick(stacked, y, 1)], []
    for d in range(4):
        part = near[0] if d == 0 else pick(stacked, (y + d) % 4, 1)
        if d > 0:
            near.append(moved(part, y=d))
        far.append(moved(part[1:], y=d, z_lo=1))
    length = lengths[0]
    block_of = [((y - c) % 4) * 2 + (z_lo if c < 4 else 1 - z_lo) for c in range(8)]
    limits = jnp.stack([length - 256 * block for block in block_of]).astype(jnp.int32)
    *out_low, out_full, log_total = forward_attention(limits, near, far)

    def in_order(parts):
        blocks = jnp.stack(parts + parts)
        return lax.dynamic_slice_in_dim(blocks, (4 - y) % 4, 4, 0)

    attended = in_order([out_low[0]] + [moved(out_low[d], y=4 - d) for d in (1, 2, 3)])
    attended = attended.reshape(width, 256)

    def rest_block(first, rows=48):
        return rest[:, first : first + rows].reshape(SHARD * rows, width)

    def rest_vector(first, count=48):
        return rest[:, 432, first : first + count].reshape(SHARD * count).astype(F32)

    w_out = rest_block(0)
    w_up = [rest_block(48 + 48 * i) for i in range(4)]
    w_down = rest_block(240, 192)
    b_out, gain_one, shift_one, b_down, gain_two, shift_two = (rest_vector(48 * i) for i in range(6))
    b_up = rest_vector(288, 192)
    resid_one = x_low.astype(F32) + product("kt,kd->td", attended, w_out) + b_out
    hidden, normed_one, inverse_one = layer_norm(resid_one, gain_one, shift_one)
    hidden_low = hidden.astype(BF)
    up_all = jnp.concatenate(w_up, axis=1)
    upward = product("td,df->tf", hidden_low, up_all) + b_up
    active_low = gelu_value(upward).astype(BF)
    resid_two = hidden + product("tf,fd->td", active_low, w_down) + b_down
    mixed, normed_two, inverse_two = layer_norm(resid_two, gain_two, shift_two)
    grad_mixed = cotangent[0].astype(F32)
    grad_gain_two = jnp.sum(grad_mixed * normed_two, axis=0)
    grad_shift_two = jnp.sum(grad_mixed, axis=0)
    grad_resid_two = norm_back(grad_mixed, normed_two, inverse_two, gain_two)
    grad_down_low = grad_resid_two.astype(BF)
    grad_b_down = jnp.sum(grad_resid_two, axis=0)
    grad_upward = product("td,fd->tf", grad_down_low, w_down) * gelu_slope(upward)
    grad_up_low = grad_upward.astype(BF)
    grad_b_up = jnp.sum(grad_upward, axis=0)
    grad_hidden = grad_resid_two + product("tf,df->td", grad_up_low, up_all)
    grad_gain_one = jnp.sum(grad_hidden * normed_one, axis=0)
    grad_shift_one = jnp.sum(grad_hidden, axis=0)
    grad_resid_one = norm_back(grad_hidden, normed_one, inverse_one, gain_one)
    grad_out_low = grad_resid_one.astype(BF)
    grad_b_out = jnp.sum(grad_resid_one, axis=0)
    grad_attended = product("kd,td->kt", w_out, grad_out_low).astype(BF).reshape(4, GROUP, HD, 256)

    grads = [pick(grad_attended, y)]
    for d in (1, 2, 3):
        grads.append(moved(pick(grad_attended, (y + d) % 4), y=d))
    grad_msgs = backward_attention(limits, near, far, grads, out_full, log_total)

    def by_shard(grad):
        return grad.astype(BF).reshape(SHARD, -1, width)

    early = jnp.concatenate(
        [by_shard(product("kt,td->kd", attended, grad_out_low))]
        + [
            by_shard(product("td,tf->df", hidden_low, grad_up_low[:, width * i : width * (i + 1)]))
            for i in range(4)
        ]
        + [by_shard(product("tf,td->fd", active_low, grad_down_low))]
        + [
            vector_rows(
                [
                    v.reshape(SHARD, -1)
                    for v in (
                        grad_b_out,
                        grad_gain_one,
                        grad_shift_one,
                        grad_b_down,
                        grad_gain_two,
                        grad_shift_two,
                        grad_b_up,
                    )
                ]
            )
        ],
        axis=1,
    )
    early = sum_over_all(early, True, place_now).astype(F32)

    back_near = [grad_msgs[0]] + [moved(grad_msgs[d], y=4 - d) for d in (1, 2, 3)]
    back_far = [moved(grad_msgs[4 + d], y=(4 - d) % 4, z_lo=1) for d in range(4)]
    finished = []
    for d in range(4):
        from_far = jnp.pad(back_far[d], [(1, 0), (0, 0), (0, 0), (0, 0)])
        finished.append(back_near[d].astype(F32) + from_far.astype(F32))
    grad_qkv = in_order(finished)
    grad_qkv = grad_qkv.transpose(1, 0, 2, 3, 4).reshape(3, width, 256)
    grad_b_query = jnp.sum(grad_qkv[0], axis=1)
    grad_b_value = jnp.sum(grad_qkv[2], axis=1)
    grad_qkv_low = grad_qkv.astype(BF)
    late = jnp.concatenate(
        [by_shard(product("td,kt->dk", x_low, grad_qkv_low[i])) for i in range(3)]
        + [vector_rows([grad_b_query.reshape(SHARD, -1), grad_b_value.reshape(SHARD, -1)])],
        axis=1,
    )
    late = sum_over_all(late, False, place_now).astype(F32)
    grad_tokens = grad_resid_one
    for i in range(3):
        grad_tokens = grad_tokens + product("kt,dk->td", grad_qkv_low[i], w_parts[i])

    def early_vector(first, count=48):
        return early[432, first : first + count]

    return (
        mixed.astype(BF)[None],
        grad_tokens[None],
        jnp.concatenate([late[48 * i : 48 * i + 48] for i in range(3)], axis=1),
        late[144, 0:48],
        late[144, 48:96],
        early[0:48],
        early_vector(0),
        early_vector(48),
        early_vector(96),
        jnp.concatenate([early[48 + 48 * i : 96 + 48 * i] for i in range(4)], axis=1),
        early_vector(288, 192),
        early[240:432],
        early_vector(144),
        early_vector(192),
        early_vector(240),
    )


def solution(mesh):
    rows, vector = P("shard", None), P("shard")
    tokens = P("shard", "ctx", None)
    return jax.shard_map(
        local,
        mesh=mesh,
        in_specs=(
            tokens, vector, tokens, rows, vector, vector, rows, vector, vector, vector,
            rows, vector, rows, vector, vector, vector,
        ),
        out_specs=(
            tokens, tokens, rows, vector, vector, rows, vector, vector, vector, rows,
            vector, rows, vector, vector, vector,
        ),
        check_vma=False,
    )
```

```python
import jax
import jax.numpy as jnp
from jax import lax
from jax.experimental import pallas as pl
from jax.experimental.pallas import tpu as pltpu
from jax.sharding import PartitionSpec as P

H = 12
HD = 64
GROUP = 3
CTX = 8
SHARD = 16
AXES = ("ctx", "shard")
EPS = 1e-12
NEG = -1e30
SCALE = HD ** (-0.5)
BF = jnp.bfloat16
F32 = jnp.float32


def place(device):
    ctx, shard = divmod(device, SHARD)
    return [shard // 4, ctx // 2, (shard // 2) % 2, ctx % 2, shard % 2]


def device_at(x, y, z_hi, z_lo, core):
    return (y * 2 + z_lo) * SHARD + x * 4 + z_hi * 2 + core


def moved(value, x=0, y=0, z_hi=0, z_lo=0, core=0):
    pairs = []
    for source in range(CTX * SHARD):
        a, b, c, d, e = place(source)
        target = device_at((a + x) % 4, (b + y) % 4, (c + z_hi) % 2, (d + z_lo) % 2, (e + core) % 2)
        pairs.append((source, target))
    return lax.ppermute(value, AXES, pairs)


def groups_along(*axes):
    found = {}
    for device in range(CTX * SHARD):
        at = place(device)
        key = tuple(v for i, v in enumerate(at) if i not in axes)
        found.setdefault(key, []).append((tuple(at[i] for i in axes), device))
    return [[d for _, d in sorted(members)] for members in found.values()]


def exchanged(blocks, *axes):
    return lax.all_to_all(blocks, AXES, 0, 0, axis_index_groups=groups_along(*axes))


def gathered(block, *axes):
    count = len(groups_along(*axes)[0])
    return exchanged(jnp.broadcast_to(block[None], (count, *block.shape)), *axes)


def total(blocks, dim=0):
    return jnp.sum(blocks.astype(F32), axis=dim)


def pick(blocks, index, dim=0):
    return lax.dynamic_index_in_dim(blocks, index, dim, keepdims=False)


def brought(pairs, sems):
    copies = [pltpu.make_async_copy(source, to, sems.at[i]) for i, (source, to) in enumerate(pairs)]
    for copy in copies:
        copy.start()
    for copy in copies:
        copy.wait()


def with_rows(block, rows):
    at = lax.broadcasted_iota(jnp.int32, (16, block.shape[1]), 0)
    extra = jnp.zeros((16, block.shape[1]), F32)
    for place_, row in enumerate(rows):
        extra = jnp.where(at == place_, row, extra)
    rest = jnp.zeros((48, block.shape[1]), BF)
    return jnp.concatenate([block, extra.astype(BF), rest], axis=0)


def turned(block):
    return block.astype(F32).T.astype(BF)


def live_row(limit):
    tokens = lax.broadcasted_iota(jnp.int32, (1, 256), 1)
    return jnp.where(tokens < limit, 0.0, NEG)


def forward_kernel(limits, *refs):
    out_low, out_full, log_total = refs[8:12], refs[12], refs[13]
    key_scr, value_scr, near_scr, far_scr, sems = refs[14:19]
    h = pl.program_id(0)

    @pl.when(h == 0)
    def _():
        pairs = [(refs[d], near_scr.at[d]) for d in range(4)]
        brought(pairs + [(refs[4 + d], far_scr.at[d]) for d in range(4)], sems)

    ones = jnp.ones((1, 256), F32)
    for c in range(8):
        keys = near_scr[c, 1, h] if c < 4 else far_scr[c - 4, 0, h]
        values = near_scr[c, 2, h] if c < 4 else far_scr[c - 4, 1, h]
        key_scr[c] = turned(with_rows(keys, [live_row(limits[c])]))
        value_scr[c] = with_rows(values, [ones])[:80]
    for b in range(4):
        queries = with_rows((near_scr[b, 0, h].astype(F32) * SCALE).astype(BF), [ones])
        scores = [
            jnp.dot(key_scr[c], queries, preferred_element_type=F32) for c in range(8)
        ]
        top = scores[0]
        for c in range(1, 8):
            top = jnp.maximum(top, scores[c])
        row_max = jnp.max(top, axis=0, keepdims=True)
        out = jnp.zeros((80, 256), F32)
        for c in range(8):
            weights = jnp.exp(scores[c] - row_max).astype(BF)
            out = out + jnp.dot(value_scr[c], weights, preferred_element_type=F32)
        row_total = out[64:65]
        attended = out[:64] / row_total
        out_low[b][0] = attended.astype(BF)
        out_full[0, b] = attended
        log_total[0, b : b + 1] = row_max + jnp.log(row_total)


ARRIVED = [
    pltpu.VMEM((4, 3, GROUP, HD, 256), BF),
    pltpu.VMEM((4, 2, GROUP, HD, 256), BF),
    pltpu.SemaphoreType.DMA((14,)),
]


def forward_attention(limits, near, far):
    return pl.pallas_call(
        forward_kernel,
        grid=(GROUP,),
        in_specs=[pl.BlockSpec(memory_space=pltpu.SMEM)] + [pl.BlockSpec(memory_space=pltpu.HBM)] * 8,
        out_specs=[pl.BlockSpec((1, HD, 256), lambda h: (h, 0, 0))] * 4
        + [
            pl.BlockSpec((1, 4, HD, 256), lambda h: (h, 0, 0, 0)),
            pl.BlockSpec((1, 4, 256), lambda h: (h, 0, 0)),
        ],
        out_shape=[jax.ShapeDtypeStruct((GROUP, HD, 256), BF)] * 4
        + [
            jax.ShapeDtypeStruct((GROUP, 4, HD, 256), F32),
            jax.ShapeDtypeStruct((GROUP, 4, 256), F32),
        ],
        scratch_shapes=[pltpu.VMEM((8, 256, 128), BF), pltpu.VMEM((8, 80, 256), BF)] + ARRIVED,
        compiler_params=pltpu.CompilerParams(vmem_limit_bytes=60 * 2**20),
        cost_estimate=pl.CostEstimate(
            flops=12 * 2048 * 256 * 512, bytes_accessed=6 * 2**20, transcendentals=12 * 2048 * 256
        ),
        name="attention_forward",
    )(limits, *near, *far)


def split_rows(row, count):
    parts = []
    for _ in range(count):
        part = row.astype(BF).astype(F32)
        parts.append(part)
        row = row - part
    return parts


def backward_kernel(limits, *refs):
    grad_near, grad_far = refs[14:18], refs[18:22]
    query_scr, query_turned, grad_scr, grad_turned = refs[22:26]
    near_scr, far_scr, sems, grads_in, out_full, log_total = refs[26:32]
    h = pl.program_id(0)

    @pl.when(h == 0)
    def _():
        pairs = [(refs[d], near_scr.at[d]) for d in range(4)]
        pairs += [(refs[4 + d], far_scr.at[d]) for d in range(4)]
        pairs += [(refs[8 + d], grads_in.at[d]) for d in range(4)]
        brought(pairs + [(refs[12], out_full), (refs[13], log_total)], sems)

    ones = jnp.ones((1, 256), F32)
    for b in range(4):
        at = slice(256 * b, 256 * b + 256)
        log_rows = split_rows(-log_total[h, b : b + 1], 3)
        queries = with_rows((near_scr[b, 0, h].astype(F32) * SCALE).astype(BF), [ones] + log_rows)
        query_scr[:, at] = queries
        query_turned[at, :] = turned(queries)
        delta = jnp.sum(grads_in[b, h].astype(F32) * out_full[h, b], axis=0, keepdims=True)
        grad = with_rows(grads_in[b, h], split_rows(-delta, 2))
        grad_scr[:, at] = grad
        grad_turned[at, :] = turned(grad)
    grad_queries = jnp.zeros((HD, 1024), F32)
    for c in range(8):
        keys = near_scr[c, 1, h] if c < 4 else far_scr[c - 4, 0, h]
        values = near_scr[c, 2, h] if c < 4 else far_scr[c - 4, 1, h]
        key_rows = turned(with_rows(keys, [live_row(limits[c]), ones, ones, ones]))
        value_rows = turned(with_rows(values, [ones, ones]))
        weights = jnp.exp(jnp.dot(key_rows, query_scr[...], preferred_element_type=F32))
        grad_soft = jnp.dot(value_rows, grad_scr[...], preferred_element_type=F32)
        grad_scores = (weights * grad_soft).astype(BF)
        grad_values = jnp.dot(weights.astype(BF), grad_turned[...], preferred_element_type=F32)
        grad_keys = jnp.dot(grad_scores, query_turned[...], preferred_element_type=F32)
        grad_queries = grad_queries + jnp.dot(keys, grad_scores, preferred_element_type=F32)
        to, first = (grad_near[c], 1) if c < 4 else (grad_far[c - 4], 0)
        to[first, 0] = grad_keys.T[:HD].astype(BF)
        to[first + 1, 0] = grad_values.T[:HD].astype(BF)
    for b in range(4):
        grad_near[b][0, 0] = (grad_queries[:, 256 * b : 256 * b + 256] * SCALE).astype(BF)


def backward_attention(limits, near, far, grads, out_full, log_total):
    head = lambda h: (0, h, 0, 0)
    near_spec = pl.BlockSpec((3, 1, HD, 256), head)
    far_spec = pl.BlockSpec((2, 1, HD, 256), head)
    return pl.pallas_call(
        backward_kernel,
        grid=(GROUP,),
        in_specs=[pl.BlockSpec(memory_space=pltpu.SMEM)] + [pl.BlockSpec(memory_space=pltpu.HBM)] * 14,
        out_specs=[near_spec] * 4 + [far_spec] * 4,
        out_shape=[jax.ShapeDtypeStruct((3, GROUP, HD, 256), BF)] * 4
        + [jax.ShapeDtypeStruct((2, GROUP, HD, 256), BF)] * 4,
        scratch_shapes=[
            pltpu.VMEM((128, 1024), BF),
            pltpu.VMEM((1024, 128), BF),
            pltpu.VMEM((128, 1024), BF),
            pltpu.VMEM((1024, 128), BF),
        ]
        + ARRIVED
        + [
            pltpu.VMEM((4, GROUP, HD, 256), BF),
            pltpu.VMEM((GROUP, 4, HD, 256), F32),
            pltpu.VMEM((GROUP, 4, 256), F32),
        ],
        compiler_params=pltpu.CompilerParams(vmem_limit_bytes=60 * 2**20),
        cost_estimate=pl.CostEstimate(
            flops=12 * 2048 * 256 * 1280, bytes_accessed=12 * 2**20, transcendentals=12 * 2048 * 256
        ),
        name="attention_backward",
    )(limits, *near, *far, *grads, out_full, log_total)


def pack_kernel(w_qkv, vectors, w_out, w_up, w_down, qkv_out, rest_out):
    qkv_out[:, :2304] = w_qkv[...]
    qkv_out[0:16, 2304:] = vectors[...]
    qkv_out[16:48, 2304:] = jnp.zeros((32, 128), BF)
    rest_out[0:48] = w_out[...]
    for i in range(4):
        rest_out[48 + 48 * i : 96 + 48 * i] = w_up[:, 768 * i : 768 * (i + 1)]
    rest_out[240:432] = w_down[...]


def packed(w_qkv, vectors, w_out, w_up, w_down):
    return pl.pallas_call(
        pack_kernel,
        out_shape=[jax.ShapeDtypeStruct((48, 2432), BF), jax.ShapeDtypeStruct((432, 768), BF)],
        name="pack_parameters",
    )(w_qkv, vectors, w_out, w_up, w_down)


def gather_pieces(own):
    other = moved(own, z_hi=1, z_lo=1)
    found = {(0, 0): own, (0, 1): other}
    for d in (1, 3, 2):
        found[d, 0] = moved(own, x=d)
    for d in (1, 3, 2):
        found[d, 1] = moved(other, x=d)
    pieces = []
    for d in range(4):
        for z in range(2):
            pieces += [found[d, z], moved(found[d, z], core=1)]
    return pieces


def shard_of(coords, d, z, c):
    x, z_hi, core = coords[0], coords[2], coords[3]
    return ((x - d + 4) % 4) * 4 + ((z_hi + z) % 2) * 2 + (core + c) % 2


PIECES = [(d, z, c) for d in range(4) for z in range(2) for c in range(2)]


def spread(vectors, row, into, at):
    wide = into.shape[1]
    lanes = lax.broadcasted_iota(jnp.int32, (8, wide), 1)
    result = jnp.broadcast_to(into, (8, wide))
    for s in range(16):
        values = jnp.broadcast_to(vectors[s][row : row + 1], (8, 128))
        values = jnp.concatenate([values, jnp.zeros((8, wide - 128), F32)], axis=1)
        first = at(s)
        if first:
            values = pltpu.roll(values, first, 1)
        result = jnp.where(jnp.logical_and(lanes >= first, lanes < first + 48), values, result)
    return result[0:1]


def project_kernel(coords, x_low, *refs):
    pieces, near, far, w_out, narrow, wide = refs[0:16], refs[16:20], refs[20:24], refs[24], refs[25], refs[26]
    vec_scr, out_scr = refs[27], refs[28]
    for piece, (d, z, c) in zip(pieces, PIECES):
        shard = shard_of(coords, d, z, c)
        w_out[pl.ds(pl.multiple_of(shard * 48, 16), 48), :] = piece[:, :2304]
        vec_scr[shard] = piece[0:16, 2304:].astype(F32)
    nothing = jnp.zeros((1, 768), F32)
    biases = [spread(vec_scr, 0, nothing, lambda s: 48 * s), None, spread(vec_scr, 1, nothing, lambda s: 48 * s)]
    for i in range(6):
        narrow[i : i + 1] = spread(vec_scr, 2 + i, nothing, lambda s: 48 * s)
    up_row = jnp.zeros((1, 3072), F32)
    for i in range(4):
        up_row = spread(vec_scr, 8 + i, up_row, lambda s: 192 * s + 48 * i)
    wide[...] = up_row
    for i in range(3):
        part = jnp.dot(x_low[...], w_out[:, 768 * i : 768 * (i + 1)], preferred_element_type=F32)
        if biases[i] is not None:
            part = part + biases[i]
        part = part.T.astype(BF)
        for g in range(4):
            for h in range(GROUP):
                at = 192 * g + 64 * h
                out_scr[g, i, h] = part[at : at + 64]
    y = coords[1]
    for d in range(4):
        group = (y + d) % 4
        near[d][...] = out_scr[group]
        far[d][...] = out_scr[group, 1:3]


def project(coords, x_low, pieces):
    outs = pl.pallas_call(
        project_kernel,
        in_specs=[pl.BlockSpec(memory_space=pltpu.SMEM)] + [pl.BlockSpec(memory_space=pltpu.VMEM)] * 17,
        out_shape=[jax.ShapeDtypeStruct((3, GROUP, HD, 256), BF)] * 4
        + [jax.ShapeDtypeStruct((2, GROUP, HD, 256), BF)] * 4
        + [
            jax.ShapeDtypeStruct((768, 2304), BF),
            jax.ShapeDtypeStruct((6, 768), F32),
            jax.ShapeDtypeStruct((1, 3072), F32),
        ],
        scratch_shapes=[pltpu.VMEM((16, 16, 128), F32), pltpu.VMEM((4, 3, GROUP, HD, 256), BF)],
        compiler_params=pltpu.CompilerParams(vmem_limit_bytes=14 * 2**20),
        cost_estimate=pl.CostEstimate(
            flops=2 * 256 * 768 * 2304, bytes_accessed=10 * 2**20, transcendentals=0
        ),
        name="project",
    )(coords, x_low, *pieces)
    return outs[0:4], outs[4:8], outs[8], outs[9], outs[10]


def unpack_kernel(rest, w_out, w_up, w_down):
    for s in range(4):
        rows = slice(48 * s, 48 * s + 48)
        w_out[rows] = rest[s, 0:48]
        for i in range(4):
            w_up[rows, 768 * i : 768 * (i + 1)] = rest[s, 48 + 48 * i : 96 + 48 * i]
        w_down[192 * s : 192 * s + 192] = rest[s, 240:432]


def unpacked(rest):
    return pl.pallas_call(
        unpack_kernel,
        grid=(4,),
        in_specs=[pl.BlockSpec((4, 432, 768), lambda i: (i, 0, 0))],
        out_specs=[
            pl.BlockSpec((192, 768), lambda i: (i, 0)),
            pl.BlockSpec((192, 3072), lambda i: (i, 0)),
            pl.BlockSpec((768, 768), lambda i: (i, 0)),
        ],
        out_shape=[
            jax.ShapeDtypeStruct((768, 768), BF),
            jax.ShapeDtypeStruct((768, 3072), BF),
            jax.ShapeDtypeStruct((3072, 768), BF),
        ],
        compiler_params=pltpu.CompilerParams(vmem_limit_bytes=14 * 2**20),
        cost_estimate=pl.CostEstimate(flops=0, bytes_accessed=22 * 2**20, transcendentals=0),
        name="unpack_parameters",
    )(rest)


def collect(row, count, first, into):
    wide = row.shape[1]
    lanes = lax.broadcasted_iota(jnp.int32, (8, 768), 1)
    full = jnp.broadcast_to(row, (8, wide))
    inside = jnp.logical_and(lanes >= first, lanes < first + count)
    for s in range(16):
        shift = (first - s * count) % wide
        turned_row = pltpu.roll(full, shift, 1) if shift else full
        into[s] = jnp.where(inside, turned_row[:, :768], into[s])


def late_kernel(coords, x_low, *refs):
    mine, send, grad_out, scr, grad_scr, vec_scr, near, far, sems, x_scr = refs[8:18]
    y, core = coords[1], coords[3]
    pairs = [(refs[d], near.at[d]) for d in range(4)] + [(refs[4 + d], far.at[d]) for d in range(4)]
    brought(pairs + [(x_low, x_scr)], sems)
    for d in range(4):
        group = (y + d) % 4
        for i in range(3):
            for h in range(GROUP):
                part = near[d, i, h].astype(F32)
                if i > 0:
                    part = part + far[d, i - 1, h].astype(F32)
                grad_scr[i, group, h] = part
    vec_scr[...] = jnp.zeros((16, 8, 768), F32)
    for i in range(3):
        block = jnp.concatenate([grad_scr[i, g, h] for g in range(4) for h in range(GROUP)], axis=0)
        block = block.T
        if i != 1:
            collect(jnp.sum(block, axis=0, keepdims=True), 48, 0 if i == 0 else 48, vec_scr)
        low = block.astype(BF)
        grad_out[:, 768 * i : 768 * (i + 1)] = low
        weights = lax.dot_general(x_scr[...], low, (((0,), (0,)), ((), ())), preferred_element_type=F32)
        weights = weights.astype(BF)
        for s in range(16):
            scr[s // 2, s % 2, 48 * i : 48 * i + 48] = weights[48 * s : 48 * s + 48]
    for s in range(16):
        row = jnp.concatenate([vec_scr[s], jnp.zeros((8, 768), F32)], axis=0)
        scr[s // 2, s % 2, 144:160] = row.astype(BF)
    for u in range(8):
        mine[u] = scr[u, core]
        send[u] = scr[u, 1 - core]


def late_gradients(coords, x_low, near, far):
    return pl.pallas_call(
        late_kernel,
        in_specs=[pl.BlockSpec(memory_space=pltpu.SMEM)] + [pl.BlockSpec(memory_space=pltpu.HBM)] * 9,
        out_shape=[
            jax.ShapeDtypeStruct((8, 160, 768), BF),
            jax.ShapeDtypeStruct((8, 160, 768), BF),
            jax.ShapeDtypeStruct((256, 2304), BF),
        ],
        scratch_shapes=[
            pltpu.VMEM((8, 2, 160, 768), BF),
            pltpu.VMEM((3, 4, GROUP, HD, 256), F32),
            pltpu.VMEM((16, 8, 768), F32),
        ]
        + ARRIVED
        + [pltpu.VMEM((256, 768), BF)],
        compiler_params=pltpu.CompilerParams(vmem_limit_bytes=24 * 2**20),
        cost_estimate=pl.CostEstimate(
            flops=2 * 256 * 768 * 2304, bytes_accessed=10 * 2**20, transcendentals=0
        ),
        name="late_gradients",
    )(coords, x_low, *near, *far)


def store_split(first, mine, send, unit, at, height, rows):
    even, odd = rows[:height], rows[height:]
    mine[unit, at : at + height] = jnp.where(first, even, odd).astype(BF)
    send[unit, at : at + height] = jnp.where(first, odd, even).astype(BF)


def down_kernel(coords, active_in, grad_in, mine, send, sems, active, grad_down):
    brought([(active_in, active), (grad_in, grad_down)], sems)
    first = coords[3] == 0
    for i in range(4):
        weights = lax.dot_general(
            active[:, 768 * i : 768 * (i + 1)],
            grad_down[...],
            (((0,), (0,)), ((), ())),
            preferred_element_type=F32,
        )
        for u in range(2):
            store_split(first, mine, send, 2 * i + u, 0, 192, weights[384 * u : 384 * u + 384])


def up_kernel(coords, *refs):
    mine, send, vec_scr, sems = refs[6:10]
    brought(list(zip(refs[0:6], refs[10:16])), sems)
    attended, hidden, grad_out, grad_up, narrow, wide = refs[10:16]
    first = coords[3] == 0
    hidden_turned = hidden[...].astype(F32).T.astype(BF)
    for i in range(4):
        weights = jnp.dot(
            hidden_turned, grad_up[:, 768 * i : 768 * (i + 1)], preferred_element_type=F32
        )
        for u in range(8):
            store_split(first, mine, send, u, 48 + 48 * i, 48, weights[96 * u : 96 * u + 96])
    weights = jnp.dot(attended[...], grad_out[...], preferred_element_type=F32)
    for u in range(8):
        store_split(first, mine, send, u, 0, 48, weights[96 * u : 96 * u + 96])
    vec_scr[...] = jnp.zeros((16, 8, 768), F32)
    for i in range(6):
        collect(narrow[i : i + 1], 48, 48 * i, vec_scr)
    collect(wide[...], 192, 288, vec_scr)
    nothing = jnp.zeros((8, 768), F32)
    for u in range(8):
        rows = jnp.concatenate([vec_scr[2 * u], nothing, vec_scr[2 * u + 1], nothing], axis=0)
        store_split(first, mine, send, u, 240, 16, rows)


def split_gradients(kernel, name, rows, blocks, scratch, coords, *arrays):
    return pl.pallas_call(
        kernel,
        in_specs=[pl.BlockSpec(memory_space=pltpu.SMEM)]
        + [pl.BlockSpec(memory_space=pltpu.HBM)] * len(arrays),
        out_shape=[jax.ShapeDtypeStruct((8, rows, 768), BF)] * 2,
        scratch_shapes=scratch,
        compiler_params=pltpu.CompilerParams(vmem_limit_bytes=20 * 2**20),
        cost_estimate=pl.CostEstimate(
            flops=2 * 256 * 768 * 768 * blocks, bytes_accessed=2 * 2**20 * blocks, transcendentals=0
        ),
        name=name,
    )(coords, *arrays)


def gelu_value(upward):
    return 0.5 * upward * (1.0 + lax.erf(upward * 0.7071067811865476))


def gelu_slope(upward):
    return (
        0.5 * (1.0 + lax.erf(upward * 0.7071067811865476))
        + upward * jnp.exp(-0.5 * upward * upward) * 0.3989422804014327
    )


def layer_norm(resid, gain, shift):
    mean = jnp.mean(resid, axis=-1, keepdims=True)
    centered = resid - mean
    spread = jnp.mean(centered * centered, axis=-1, keepdims=True)
    inverse = lax.rsqrt(spread + EPS)
    normed = centered * inverse
    return (normed * gain + shift, normed, inverse)


def norm_back(grad_out, normed, inverse, gain):
    grad_normed = grad_out * gain
    return inverse * (
        grad_normed
        - jnp.mean(grad_normed, axis=-1, keepdims=True)
        - normed * jnp.mean(grad_normed * normed, axis=-1, keepdims=True)
    )


def product(spec, left, right):
    return jnp.einsum(spec, left, right, preferred_element_type=F32)


def add(left, right):
    return (left.astype(F32) + right.astype(F32)).astype(BF)


def finish_sum(mine):
    mine = add(mine, moved(mine, z_lo=1))
    return gathered(mine, 1)


def core_sum(mine, send):
    return add(mine, moved(send, core=1))


def along_x(units):
    return total(exchanged(units.reshape(4, 2, *units.shape[1:]), 0)).astype(BF)


def along_y(quarters, y):
    mine = pick(quarters, y).astype(F32)
    for d in (1, 3, 2):
        mine = mine + moved(pick(quarters, (y + d) % 4), y=d).astype(F32)
    return mine.astype(BF)


def early_sum(own, place_now):
    x, y, z_hi, core = place_now
    rows = own.shape[1]
    partial = add(pick(own, z_hi), moved(pick(own, 1 - z_hi), z_hi=1, z_lo=1))
    return along_y(partial.reshape(4, rows // 4, 768), y)


def finish_kernel(owned, w_qkv, w_out, w_up, w_down, vectors):
    late = jnp.concatenate([owned[q].astype(F32)[:40] for q in range(4)], axis=0)
    early = jnp.concatenate([owned[q].astype(F32)[40:] for q in range(4)], axis=0)
    for i in range(3):
        w_qkv[:, 768 * i : 768 * (i + 1)] = late[48 * i : 48 * i + 48]
    w_out[...] = early[0:48]
    for i in range(4):
        w_up[:, 768 * i : 768 * (i + 1)] = early[48 + 48 * i : 96 + 48 * i]
    w_down[...] = early[256:448]
    vectors[0:8] = late[144:152]
    vectors[8:16] = early[240:248]


def finished(owned):
    shapes = [(48, 2304), (48, 768), (48, 3072), (192, 768), (16, 768)]
    return pl.pallas_call(
        finish_kernel,
        out_shape=[jax.ShapeDtypeStruct(shape, F32) for shape in shapes],
        name="finish_gradients",
    )(owned)


def late_sum(units, y):
    rows = units.shape[1]
    units = along_y(units.reshape(8, 4, rows // 4, 768).transpose(1, 0, 2, 3), y)
    return total(exchanged(units, 0, 2)).astype(BF)


def local(
    tokens,
    lengths,
    cotangent,
    w_qkv,
    b_query,
    b_value,
    w_out,
    b_out,
    gain_one,
    shift_one,
    w_up,
    b_up,
    w_down,
    b_down,
    gain_two,
    shift_two,
):
    ctx, shard = lax.axis_index("ctx"), lax.axis_index("shard")
    y, z_lo = ctx // 2, ctx % 2
    x, z_hi, core = shard // 4, (shard // 2) % 2, shard % 2
    place_now = (x, y, z_hi, core)
    width = 768
    x_low = tokens[0]

    coords = jnp.stack([x, y, z_hi, core]).astype(jnp.int32)
    vectors = jnp.stack([b_query, b_value, b_out, gain_one, shift_one, b_down, gain_two, shift_two])
    vectors = jnp.concatenate([vectors, b_up.reshape(4, 48)], axis=0)
    vectors = jnp.pad(vectors, [(0, 4), (0, 80)])
    qkv_own, rest_own = packed(w_qkv, vectors, w_out, w_up, w_down)
    rest = lax.all_gather(rest_own, "shard", axis=0, tiled=True)
    qkv_pieces = gather_pieces(qkv_own)

    near_send, far_send, w_qkv, narrow, b_up = project(coords, x_low, qkv_pieces)
    far = [moved(far_send[d], y=d, z_lo=1) for d in (2, 1, 3, 0)]
    far = [far[3], far[1], far[0], far[2]]
    near = [near_send[0]] + [moved(near_send[d], y=d) for d in (1, 2, 3)]
    length = lengths[0]
    block_of = [((y - c) % 4) * 2 + (z_lo if c < 4 else 1 - z_lo) for c in range(8)]
    limits = jnp.stack([length - 256 * block for block in block_of]).astype(jnp.int32)
    *out_low, out_full, log_total = forward_attention(limits, near, far)
    _, rest = lax.optimization_barrier((out_low[0], rest))

    def in_order(parts):
        blocks = jnp.stack(parts + parts)
        return lax.dynamic_slice_in_dim(blocks, (4 - y) % 4, 4, 0)

    attended = in_order([out_low[0]] + [moved(out_low[d], y=4 - d) for d in (1, 2, 3)])
    attended = attended.reshape(width, 256)

    w_out, up_all, w_down = unpacked(rest.reshape(SHARD, 432, width))
    b_out, gain_one, shift_one, b_down, gain_two, shift_two = (narrow[i] for i in range(6))
    resid_one = x_low.astype(F32) + product("kt,kd->td", attended, w_out) + b_out
    hidden, normed_one, inverse_one = layer_norm(resid_one, gain_one, shift_one)
    hidden_low = hidden.astype(BF)
    upward = product("td,df->tf", hidden_low, up_all) + b_up
    active_low = gelu_value(upward).astype(BF)
    resid_two = hidden + product("tf,fd->td", active_low, w_down) + b_down
    mixed, normed_two, inverse_two = layer_norm(resid_two, gain_two, shift_two)
    grad_mixed = cotangent[0].astype(F32)
    grad_gain_two = jnp.sum(grad_mixed * normed_two, axis=0)
    grad_shift_two = jnp.sum(grad_mixed, axis=0)
    grad_resid_two = norm_back(grad_mixed, normed_two, inverse_two, gain_two)
    grad_down_low = grad_resid_two.astype(BF)
    grad_b_down = jnp.sum(grad_resid_two, axis=0)
    down_split = split_gradients(
        down_kernel,
        "down_gradients",
        192,
        4,
        [pltpu.SemaphoreType.DMA((2,)), pltpu.VMEM((256, 3072), BF), pltpu.VMEM((256, 768), BF)],
        coords,
        active_low,
        grad_down_low,
    )
    down_units = core_sum(*down_split)
    grad_upward = product("td,fd->tf", grad_down_low, w_down) * gelu_slope(upward)
    grad_up_low = grad_upward.astype(BF)
    grad_b_up = jnp.sum(grad_upward, axis=0)
    grad_hidden = grad_resid_two + product("tf,df->td", grad_up_low, up_all)
    grad_gain_one = jnp.sum(grad_hidden * normed_one, axis=0)
    grad_shift_one = jnp.sum(grad_hidden, axis=0)
    grad_resid_one = norm_back(grad_hidden, normed_one, inverse_one, gain_one)
    grad_out_low = grad_resid_one.astype(BF)
    grad_b_out = jnp.sum(grad_resid_one, axis=0)
    grad_attended = product("kd,td->kt", w_out, grad_out_low).astype(BF).reshape(4, GROUP, HD, 256)

    grads = [pick(grad_attended, y)]
    for d in (1, 2, 3):
        grads.append(moved(pick(grad_attended, (y + d) % 4), y=d))
    grad_narrow = jnp.stack(
        [grad_b_out, grad_gain_one, grad_shift_one, grad_b_down, grad_gain_two, grad_shift_two]
    )
    grads, down_units = lax.optimization_barrier((grads, down_units))
    down_own = along_x(down_units)
    grad_msgs = list(backward_attention(limits, near, far, grads, out_full, log_total))
    hidden_low, down_own, grad_msgs[0] = lax.optimization_barrier((hidden_low, down_own, grad_msgs[0]))
    up_split = split_gradients(
        up_kernel,
        "up_gradients",
        256,
        5,
        [
            pltpu.VMEM((16, 8, 768), F32),
            pltpu.SemaphoreType.DMA((6,)),
            pltpu.VMEM((768, 256), BF),
            pltpu.VMEM((256, 768), BF),
            pltpu.VMEM((256, 768), BF),
            pltpu.VMEM((256, 3072), BF),
            pltpu.VMEM((6, 768), F32),
            pltpu.VMEM((1, 3072), F32),
        ],
        coords,
        attended,
        hidden_low,
        grad_out_low,
        grad_up_low,
        grad_narrow,
        grad_b_up[None],
    )
    up_units = core_sum(*up_split)
    up_own = along_x(up_units)

    back_near = [grad_msgs[0]] + [moved(grad_msgs[d], y=4 - d) for d in (1, 2, 3)]
    back_far = [moved(grad_msgs[4 + d], y=(4 - d) % 4, z_lo=1) for d in range(4)]
    mine, send, grad_qkv = late_gradients(coords, x_low, back_near, back_far)
    units, up_own = lax.optimization_barrier((core_sum(mine, send), up_own))
    early = early_sum(jnp.concatenate([up_own, down_own], axis=1), place_now)
    late = late_sum(units, y)
    owned = finish_sum(jnp.concatenate([late, early], axis=0))
    grad_w_qkv, grad_w_out, grad_w_up, grad_w_down, vectors = finished(owned)
    grad_tokens = grad_resid_one + product("tk,dk->td", grad_qkv, w_qkv)

    def early_vector(first, count=48):
        return vectors[8, first : first + count]

    return (
        mixed.astype(BF)[None],
        grad_tokens[None],
        grad_w_qkv,
        vectors[0, 0:48],
        vectors[0, 48:96],
        grad_w_out,
        early_vector(0),
        early_vector(48),
        early_vector(96),
        grad_w_up,
        early_vector(288, 192),
        grad_w_down,
        early_vector(144),
        early_vector(192),
        early_vector(240),
    )


def solution(mesh):
    rows, vector = P("shard", None), P("shard")
    tokens = P("shard", "ctx", None)
    return jax.shard_map(
        local,
        mesh=mesh,
        in_specs=(
            tokens, vector, tokens, rows, vector, vector, rows, vector, vector, vector,
            rows, vector, rows, vector, vector, vector,
        ),
        out_specs=(
            tokens, tokens, rows, vector, vector, rows, vector, vector, vector, rows,
            vector, rows, vector, vector, vector,
        ),
        check_vma=False,
    )
```

```python
import jax
import jax.numpy as jnp
from jax import lax
from jax.experimental import pallas as pl
from jax.experimental.pallas import tpu as pltpu
from jax.sharding import PartitionSpec as P

H = 12
HD = 64
GROUP = 3
CTX = 8
SHARD = 16
AXES = ("ctx", "shard")
EPS = 1e-12
NEG = -1e30
SCALE = HD ** (-0.5)
BF = jnp.bfloat16
F32 = jnp.float32


def place(device):
    ctx, shard = divmod(device, SHARD)
    return [shard // 4, ctx // 2, (shard // 2) % 2, ctx % 2, shard % 2]


def device_at(x, y, z_hi, z_lo, core):
    return (y * 2 + z_lo) * SHARD + x * 4 + z_hi * 2 + core


def moved(value, x=0, y=0, z_hi=0, z_lo=0, core=0):
    pairs = []
    for source in range(CTX * SHARD):
        a, b, c, d, e = place(source)
        target = device_at((a + x) % 4, (b + y) % 4, (c + z_hi) % 2, (d + z_lo) % 2, (e + core) % 2)
        pairs.append((source, target))
    return lax.ppermute(value, AXES, pairs)


def groups_along(*axes):
    found = {}
    for device in range(CTX * SHARD):
        at = place(device)
        key = tuple(v for i, v in enumerate(at) if i not in axes)
        found.setdefault(key, []).append((tuple(at[i] for i in axes), device))
    return [[d for _, d in sorted(members)] for members in found.values()]


def exchanged(blocks, *axes):
    return lax.all_to_all(blocks, AXES, 0, 0, axis_index_groups=groups_along(*axes))


def gathered(block, *axes):
    count = len(groups_along(*axes)[0])
    return exchanged(jnp.broadcast_to(block[None], (count, *block.shape)), *axes)


def total(blocks, dim=0):
    return jnp.sum(blocks.astype(F32), axis=dim)


def pick(blocks, index, dim=0):
    return lax.dynamic_index_in_dim(blocks, index, dim, keepdims=False)


def brought(pairs, sems):
    copies = [pltpu.make_async_copy(source, to, sems.at[i]) for i, (source, to) in enumerate(pairs)]
    for copy in copies:
        copy.start()
    for copy in copies:
        copy.wait()


def with_rows(block, rows):
    at = lax.broadcasted_iota(jnp.int32, (16, block.shape[1]), 0)
    extra = jnp.zeros((16, block.shape[1]), F32)
    for place_, row in enumerate(rows):
        extra = jnp.where(at == place_, row, extra)
    rest = jnp.zeros((48, block.shape[1]), BF)
    return jnp.concatenate([block, extra.astype(BF), rest], axis=0)


def turned(block):
    return block.astype(F32).T.astype(BF)


def live_row(limit):
    tokens = lax.broadcasted_iota(jnp.int32, (1, 256), 1)
    return jnp.where(tokens < limit, 0.0, NEG)


def forward_kernel(limits, *refs):
    out_low, out_full, log_total = refs[8:12], refs[12], refs[13]
    key_scr, value_scr, near_scr, far_scr, sems = refs[14:19]
    h = pl.program_id(0)

    @pl.when(h == 0)
    def _():
        pairs = [(refs[d], near_scr.at[d]) for d in range(4)]
        brought(pairs + [(refs[4 + d], far_scr.at[d]) for d in range(4)], sems)

    ones = jnp.ones((1, 256), F32)
    for c in range(8):
        keys = near_scr[c, 1, h] if c < 4 else far_scr[c - 4, 0, h]
        values = near_scr[c, 2, h] if c < 4 else far_scr[c - 4, 1, h]
        key_scr[c] = turned(with_rows(keys, [live_row(limits[c])]))
        value_scr[c] = with_rows(values, [ones])[:80]
    for b in range(4):
        queries = with_rows((near_scr[b, 0, h].astype(F32) * SCALE).astype(BF), [ones])
        scores = [
            jnp.dot(key_scr[c], queries, preferred_element_type=F32) for c in range(8)
        ]
        top = scores[0]
        for c in range(1, 8):
            top = jnp.maximum(top, scores[c])
        row_max = jnp.max(top, axis=0, keepdims=True)
        out = jnp.zeros((80, 256), F32)
        for c in range(8):
            weights = jnp.exp(scores[c] - row_max).astype(BF)
            out = out + jnp.dot(value_scr[c], weights, preferred_element_type=F32)
        row_total = out[64:65]
        attended = out[:64] / row_total
        out_low[b][0] = attended.astype(BF)
        out_full[0, b] = attended
        log_total[0, b : b + 1] = row_max + jnp.log(row_total)


ARRIVED = [
    pltpu.VMEM((4, 3, GROUP, HD, 256), BF),
    pltpu.VMEM((4, 2, GROUP, HD, 256), BF),
    pltpu.SemaphoreType.DMA((14,)),
]


def forward_attention(limits, near, far):
    return pl.pallas_call(
        forward_kernel,
        grid=(GROUP,),
        in_specs=[pl.BlockSpec(memory_space=pltpu.SMEM)] + [pl.BlockSpec(memory_space=pltpu.HBM)] * 8,
        out_specs=[pl.BlockSpec((1, HD, 256), lambda h: (h, 0, 0))] * 4
        + [
            pl.BlockSpec((1, 4, HD, 256), lambda h: (h, 0, 0, 0)),
            pl.BlockSpec((1, 4, 256), lambda h: (h, 0, 0)),
        ],
        out_shape=[jax.ShapeDtypeStruct((GROUP, HD, 256), BF)] * 4
        + [
            jax.ShapeDtypeStruct((GROUP, 4, HD, 256), F32),
            jax.ShapeDtypeStruct((GROUP, 4, 256), F32),
        ],
        scratch_shapes=[pltpu.VMEM((8, 256, 128), BF), pltpu.VMEM((8, 80, 256), BF)] + ARRIVED,
        compiler_params=pltpu.CompilerParams(vmem_limit_bytes=60 * 2**20),
        cost_estimate=pl.CostEstimate(
            flops=12 * 2048 * 256 * 512, bytes_accessed=6 * 2**20, transcendentals=12 * 2048 * 256
        ),
        name="attention_forward",
    )(limits, *near, *far)


def split_rows(row, count):
    parts = []
    for _ in range(count):
        part = row.astype(BF).astype(F32)
        parts.append(part)
        row = row - part
    return parts


def backward_kernel(limits, *refs):
    grad_near, grad_far = refs[14:18], refs[18:22]
    query_scr, query_turned, grad_scr, grad_turned = refs[22:26]
    near_scr, far_scr, sems, grads_in, out_full, log_total = refs[26:32]
    h = pl.program_id(0)

    @pl.when(h == 0)
    def _():
        pairs = [(refs[d], near_scr.at[d]) for d in range(4)]
        pairs += [(refs[4 + d], far_scr.at[d]) for d in range(4)]
        pairs += [(refs[8 + d], grads_in.at[d]) for d in range(4)]
        brought(pairs + [(refs[12], out_full), (refs[13], log_total)], sems)

    ones = jnp.ones((1, 256), F32)
    for b in range(4):
        at = slice(256 * b, 256 * b + 256)
        log_rows = split_rows(-log_total[h, b : b + 1], 3)
        queries = with_rows((near_scr[b, 0, h].astype(F32) * SCALE).astype(BF), [ones] + log_rows)
        query_scr[:, at] = queries
        query_turned[at, :] = turned(queries)
        delta = jnp.sum(grads_in[b, h].astype(F32) * out_full[h, b], axis=0, keepdims=True)
        grad = with_rows(grads_in[b, h], split_rows(-delta, 2))
        grad_scr[:, at] = grad
        grad_turned[at, :] = turned(grad)
    grad_queries = jnp.zeros((HD, 1024), F32)
    for c in range(8):
        keys = near_scr[c, 1, h] if c < 4 else far_scr[c - 4, 0, h]
        values = near_scr[c, 2, h] if c < 4 else far_scr[c - 4, 1, h]
        key_rows = turned(with_rows(keys, [live_row(limits[c]), ones, ones, ones]))
        value_rows = turned(with_rows(values, [ones, ones]))
        weights = jnp.exp(jnp.dot(key_rows, query_scr[...], preferred_element_type=F32))
        grad_soft = jnp.dot(value_rows, grad_scr[...], preferred_element_type=F32)
        grad_scores = (weights * grad_soft).astype(BF)
        grad_values = jnp.dot(weights.astype(BF), grad_turned[...], preferred_element_type=F32)
        grad_keys = jnp.dot(grad_scores, query_turned[...], preferred_element_type=F32)
        grad_queries = grad_queries + jnp.dot(keys, grad_scores, preferred_element_type=F32)
        to, first = (grad_near[c], 1) if c < 4 else (grad_far[c - 4], 0)
        to[first, 0] = grad_keys.T[:HD].astype(BF)
        to[first + 1, 0] = grad_values.T[:HD].astype(BF)
    for b in range(4):
        grad_near[b][0, 0] = (grad_queries[:, 256 * b : 256 * b + 256] * SCALE).astype(BF)


def backward_attention(limits, near, far, grads, out_full, log_total):
    head = lambda h: (0, h, 0, 0)
    near_spec = pl.BlockSpec((3, 1, HD, 256), head)
    far_spec = pl.BlockSpec((2, 1, HD, 256), head)
    return pl.pallas_call(
        backward_kernel,
        grid=(GROUP,),
        in_specs=[pl.BlockSpec(memory_space=pltpu.SMEM)] + [pl.BlockSpec(memory_space=pltpu.HBM)] * 14,
        out_specs=[near_spec] * 4 + [far_spec] * 4,
        out_shape=[jax.ShapeDtypeStruct((3, GROUP, HD, 256), BF)] * 4
        + [jax.ShapeDtypeStruct((2, GROUP, HD, 256), BF)] * 4,
        scratch_shapes=[
            pltpu.VMEM((128, 1024), BF),
            pltpu.VMEM((1024, 128), BF),
            pltpu.VMEM((128, 1024), BF),
            pltpu.VMEM((1024, 128), BF),
        ]
        + ARRIVED
        + [
            pltpu.VMEM((4, GROUP, HD, 256), BF),
            pltpu.VMEM((GROUP, 4, HD, 256), F32),
            pltpu.VMEM((GROUP, 4, 256), F32),
        ],
        compiler_params=pltpu.CompilerParams(vmem_limit_bytes=60 * 2**20),
        cost_estimate=pl.CostEstimate(
            flops=12 * 2048 * 256 * 1280, bytes_accessed=12 * 2**20, transcendentals=12 * 2048 * 256
        ),
        name="attention_backward",
    )(limits, *near, *far, *grads, out_full, log_total)


def select(index, choices):
    result = choices[0]
    for i, choice in enumerate(choices[1:], 1):
        result = jnp.where(index == i, choice, result)
    return result


def pack_kernel(coords, w_qkv, vectors, qkv_out):
    whole = w_qkv[...].astype(F32)
    for i in range(3):
        choices = [whole[:, 768 * i + 192 * j : 768 * i + 192 * (j + 1)] for j in range(4)]
        part = jnp.concatenate([select(coords[1], choices), jnp.zeros((48, 64), F32)], axis=1)
        qkv_out[:, 256 * i : 256 * (i + 1)] = part.astype(BF)
    qkv_out[0:16, 768:] = vectors[...]
    qkv_out[16:48, 768:] = jnp.zeros((32, 128), BF)


def packed(coords, w_qkv, vectors):
    return pl.pallas_call(
        pack_kernel,
        in_specs=[pl.BlockSpec(memory_space=pltpu.SMEM)] + [pl.BlockSpec(memory_space=pltpu.VMEM)] * 2,
        out_shape=jax.ShapeDtypeStruct((48, 896), BF),
        name="pack_heads",
    )(coords, w_qkv, vectors)


def join_kernel(w_out, w_up, w_down, out):
    out[0:48] = w_out[...]
    for i in range(4):
        out[48 + 48 * i : 96 + 48 * i] = w_up[:, 768 * i : 768 * (i + 1)]
    out[240:432] = w_down[...]


def joined(w_out, w_up, w_down):
    return pl.pallas_call(
        join_kernel, out_shape=jax.ShapeDtypeStruct((432, 768), BF), name="join_parameters"
    )(w_out, w_up, w_down)


def spread(vectors, row, into, at):
    wide = into.shape[1]
    lanes = lax.broadcasted_iota(jnp.int32, (8, wide), 1)
    result = jnp.broadcast_to(into, (8, wide))
    for s in range(16):
        values = jnp.broadcast_to(vectors[s][row : row + 1], (8, 128))
        values = jnp.concatenate([values, jnp.zeros((8, wide - 128), F32)], axis=1)
        first = at(s)
        if first:
            values = pltpu.roll(values, first, 1)
        result = jnp.where(jnp.logical_and(lanes >= first, lanes < first + 48), values, result)
    return result[0:1]


def project_kernel(coords, *refs):
    near, far, narrow, wide = refs[5:9], refs[9:13], refs[13], refs[14]
    weights, x_all, vec_scr, sems = refs[15:19]
    brought([(refs[0], weights)] + [(refs[1 + d], x_all.at[d]) for d in range(4)], sems)
    for s in range(16):
        vec_scr[s] = weights[48 * s : 48 * s + 16, 768:].astype(F32)
    nothing = jnp.zeros((1, 768), F32)
    biases = []
    for i in range(2):
        row = jnp.broadcast_to(spread(vec_scr, i, nothing, lambda s: 48 * s), (8, 768))
        turns = [pltpu.roll(row, (768 - 192 * j) % 768, 1) if j else row for j in range(4)]
        biases.append(select(coords[1], turns)[0:1, :256])
    bias = jnp.concatenate([biases[0], jnp.zeros((1, 256), F32), biases[1]], axis=1)
    for c in range(8):
        if c < 4:
            part = jnp.dot(x_all[c, 0], weights[:, :768], preferred_element_type=F32) + bias
        else:
            part = jnp.dot(x_all[c - 4, 1], weights[:, 256:768], preferred_element_type=F32)
            part = part + bias[:, 256:]
        part = part.T.astype(BF)
        to = near[c] if c < 4 else far[c - 4]
        for i in range(3 if c < 4 else 2):
            for h in range(GROUP):
                at = 256 * i + 64 * h
                to[i, h] = part[at : at + 64]
    for i in range(6):
        narrow[i : i + 1] = spread(vec_scr, 2 + i, nothing, lambda s: 48 * s)
    up_row = jnp.zeros((1, 3072), F32)
    for i in range(4):
        up_row = spread(vec_scr, 8 + i, up_row, lambda s: 192 * s + 48 * i)
    wide[...] = up_row


def project(coords, w_heads, x_pairs):
    outs = pl.pallas_call(
        project_kernel,
        in_specs=[pl.BlockSpec(memory_space=pltpu.SMEM)] + [pl.BlockSpec(memory_space=pltpu.HBM)] * 5,
        out_shape=[jax.ShapeDtypeStruct((3, GROUP, HD, 256), BF)] * 4
        + [jax.ShapeDtypeStruct((2, GROUP, HD, 256), BF)] * 4
        + [jax.ShapeDtypeStruct((6, 768), F32), jax.ShapeDtypeStruct((1, 3072), F32)],
        scratch_shapes=[
            pltpu.VMEM((768, 896), BF),
            pltpu.VMEM((4, 2, 256, 768), BF),
            pltpu.VMEM((16, 16, 128), F32),
            pltpu.SemaphoreType.DMA((9,)),
        ],
        compiler_params=pltpu.CompilerParams(vmem_limit_bytes=60 * 2**20),
        cost_estimate=pl.CostEstimate(
            flops=2 * 2048 * 768 * 640, bytes_accessed=8 * 2**20, transcendentals=0
        ),
        name="project",
    )(coords, w_heads, *x_pairs)
    return outs[0:4], outs[4:8], outs[8], outs[9]


def unpack_kernel(coords, *refs):
    w_out, w_up, w_down = refs[4:7]
    for i, rest in enumerate(refs[0:4]):
        member = ((coords[2] + i % 2) % 2) * 2 + (coords[3] + i // 2) % 2
        rows = pl.ds(pl.multiple_of(member * 48, 16), 48)
        w_out[rows] = rest[0, 0:48]
        for i in range(4):
            w_up[rows, 768 * i : 768 * (i + 1)] = rest[0, 48 + 48 * i : 96 + 48 * i]
        w_down[pl.ds(pl.multiple_of(member * 192, 16), 192)] = rest[0, 240:432]


def unpacked(coords, *rests):
    block = pl.BlockSpec((1, 432, 768), lambda i: (i, 0, 0))
    return pl.pallas_call(
        unpack_kernel,
        grid=(4,),
        in_specs=[pl.BlockSpec(memory_space=pltpu.SMEM)] + [block] * 4,
        out_specs=[
            pl.BlockSpec((192, 768), lambda i: (i, 0)),
            pl.BlockSpec((192, 3072), lambda i: (i, 0)),
            pl.BlockSpec((768, 768), lambda i: (i, 0)),
        ],
        out_shape=[
            jax.ShapeDtypeStruct((768, 768), BF),
            jax.ShapeDtypeStruct((768, 3072), BF),
            jax.ShapeDtypeStruct((3072, 768), BF),
        ],
        compiler_params=pltpu.CompilerParams(vmem_limit_bytes=18 * 2**20),
        cost_estimate=pl.CostEstimate(flops=0, bytes_accessed=22 * 2**20, transcendentals=0),
        name="unpack_parameters",
    )(coords, *rests)


def collect(row, count, first, into):
    wide = row.shape[1]
    lanes = lax.broadcasted_iota(jnp.int32, (8, 768), 1)
    full = jnp.broadcast_to(row, (8, wide))
    inside = jnp.logical_and(lanes >= first, lanes < first + count)
    for s in range(16):
        shift = (first - s * count) % wide
        turned_row = pltpu.roll(full, shift, 1) if shift else full
        into[s] = jnp.where(inside, turned_row[:, :768], into[s])


def late_kernel(coords, *refs):
    narrow, wide, mine, send, back = refs[13], refs[14], refs[15], refs[16], refs[17:21]
    weights, x_all, near, far, sems, vec_scr = refs[21:27]
    y, first = coords[1], coords[3] == 0
    pairs = [(refs[0], weights)] + [(refs[1 + d], x_all.at[d]) for d in range(4)]
    pairs += [(refs[5 + d], near.at[d]) for d in range(4)]
    brought(pairs + [(refs[9 + d], far.at[d]) for d in range(4)], sems)
    ones = jnp.ones((256, 128), BF)
    totals, sums = [None] * 3, [None] * 3
    for c in range(8):
        back_part = jnp.zeros((768, 256), F32)
        for i in range(3):
            if c >= 4 and i == 0:
                continue
            grad = near[c, i] if c < 4 else far[c - 4, i - 1]
            grad = grad.reshape(192, 256)
            part = jnp.dot(grad, x_all[c % 4, c // 4], preferred_element_type=F32)
            row = jnp.dot(grad, ones, preferred_element_type=F32)
            totals[i] = part if totals[i] is None else totals[i] + part
            sums[i] = row if sums[i] is None else sums[i] + row
            back_part = back_part + jnp.dot(
                weights[:, 256 * i : 256 * i + 192], grad, preferred_element_type=F32
            )
        back[c % 4][c // 4] = back_part.T.astype(BF)
    gap = jnp.zeros((64, 768), F32)
    grads = jnp.concatenate([jnp.concatenate([t, gap], axis=0).T for t in totals], axis=1)
    for u in range(8):
        store_split(first, mine, send, u, 0, 48, grads[96 * u : 96 * u + 96])
    rows = []
    for i in (0, 2):
        row = jnp.concatenate([sums[i], jnp.zeros((64, 128), F32)], axis=0).T[0:8]
        rows.append(jnp.concatenate([row, jnp.zeros((8, 512), F32)], axis=1))
    lanes = lax.broadcasted_iota(jnp.int32, (8, 768), 1)
    vectors = []
    for j in range(4):
        query = pltpu.roll(rows[0], (768 - 48 * j) % 768, 1) if j else rows[0]
        shift = (768 + 48 - 48 * j) % 768
        value = pltpu.roll(rows[1], shift, 1) if shift else rows[1]
        vector = jnp.where(lanes < 48, query, jnp.where(lanes < 96, value, 0.0))
        vectors.append(vector)
    vec_scr[...] = jnp.zeros((16, 8, 768), F32)
    for i in range(6):
        collect(narrow[i : i + 1], 48, 48 * i, vec_scr)
    collect(wide[...], 192, 288, vec_scr)
    nothing = jnp.zeros((8, 768), F32)
    for u in range(8):
        both = [nothing, vec_scr[2 * u], nothing, vec_scr[2 * u + 1]]
        store_split(first, mine, send, u, 48, 16, jnp.concatenate(both, axis=0))
    for j in range(2):
        unit = 2 * y + j
        both = [vectors[2 * j], vec_scr[2 * unit], vectors[2 * j + 1], vec_scr[2 * unit + 1]]
        store_split(first, mine, send, unit, 48, 16, jnp.concatenate(both, axis=0))


def late_gradients(coords, w_heads, x_pairs, grad_msgs, narrow, wide):
    outs = pl.pallas_call(
        late_kernel,
        in_specs=[pl.BlockSpec(memory_space=pltpu.SMEM)]
        + [pl.BlockSpec(memory_space=pltpu.HBM)] * 13
        + [pl.BlockSpec(memory_space=pltpu.VMEM)] * 2,
        out_shape=[jax.ShapeDtypeStruct((8, 64, 768), BF)] * 2
        + [jax.ShapeDtypeStruct((2, 256, 768), BF)] * 4,
        scratch_shapes=[
            pltpu.VMEM((768, 896), BF),
            pltpu.VMEM((4, 2, 256, 768), BF),
            pltpu.VMEM((4, 3, GROUP, HD, 256), BF),
            pltpu.VMEM((4, 2, GROUP, HD, 256), BF),
            pltpu.SemaphoreType.DMA((17,)),
            pltpu.VMEM((16, 8, 768), F32),
        ],
        compiler_params=pltpu.CompilerParams(vmem_limit_bytes=60 * 2**20),
        cost_estimate=pl.CostEstimate(
            flops=4 * 2048 * 768 * 512, bytes_accessed=12 * 2**20, transcendentals=0
        ),
        name="late_gradients",
    )(coords, w_heads, *x_pairs, *grad_msgs, narrow, wide)
    return outs[0], outs[1], outs[2:]


def store_split(first, mine, send, unit, at, height, rows):
    even, odd = rows[:height], rows[height:]
    mine[unit, at : at + height] = jnp.where(first, even, odd).astype(BF)
    send[unit, at : at + height] = jnp.where(first, odd, even).astype(BF)


def down_kernel(coords, active_in, grad_in, mine, send, sems, active, grad_down):
    brought([(active_in, active), (grad_in, grad_down)], sems)
    first = coords[3] == 0
    for i in range(4):
        weights = lax.dot_general(
            active[:, 768 * i : 768 * (i + 1)],
            grad_down[...],
            (((0,), (0,)), ((), ())),
            preferred_element_type=F32,
        )
        for u in range(2):
            store_split(first, mine, send, 2 * i + u, 0, 192, weights[384 * u : 384 * u + 384])


def up_kernel(coords, *refs):
    mine, send, sems = refs[4:7]
    brought(list(zip(refs[0:4], refs[7:11])), sems)
    attended, hidden, grad_out, grad_up = refs[7:11]
    first = coords[3] == 0
    hidden_turned = hidden[...].astype(F32).T.astype(BF)
    for i in range(4):
        weights = jnp.dot(
            hidden_turned, grad_up[:, 768 * i : 768 * (i + 1)], preferred_element_type=F32
        )
        for u in range(8):
            store_split(first, mine, send, u, 48 + 48 * i, 48, weights[96 * u : 96 * u + 96])
    weights = jnp.dot(attended[...], grad_out[...], preferred_element_type=F32)
    for u in range(8):
        store_split(first, mine, send, u, 0, 48, weights[96 * u : 96 * u + 96])
    for u in range(8):
        mine[u, 240:256] = jnp.zeros((16, 768), BF)
        send[u, 240:256] = jnp.zeros((16, 768), BF)


def split_gradients(kernel, name, rows, blocks, scratch, coords, *arrays):
    return pl.pallas_call(
        kernel,
        in_specs=[pl.BlockSpec(memory_space=pltpu.SMEM)]
        + [pl.BlockSpec(memory_space=pl.ANY)] * len(arrays),
        out_shape=[jax.ShapeDtypeStruct((8, rows, 768), BF)] * 2,
        scratch_shapes=scratch,
        compiler_params=pltpu.CompilerParams(vmem_limit_bytes=20 * 2**20),
        cost_estimate=pl.CostEstimate(
            flops=2 * 256 * 768 * 768 * blocks, bytes_accessed=2 * 2**20 * blocks, transcendentals=0
        ),
        name=name,
    )(coords, *arrays)


def gelu_value(upward):
    return 0.5 * upward * (1.0 + lax.erf(upward * 0.7071067811865476))


def gelu_slope(upward):
    return (
        0.5 * (1.0 + lax.erf(upward * 0.7071067811865476))
        + upward * jnp.exp(-0.5 * upward * upward) * 0.3989422804014327
    )


def layer_norm(resid, gain, shift):
    mean = jnp.mean(resid, axis=-1, keepdims=True)
    centered = resid - mean
    spread = jnp.mean(centered * centered, axis=-1, keepdims=True)
    inverse = lax.rsqrt(spread + EPS)
    normed = centered * inverse
    return (normed * gain + shift, normed, inverse)


def norm_back(grad_out, normed, inverse, gain):
    grad_normed = grad_out * gain
    return inverse * (
        grad_normed
        - jnp.mean(grad_normed, axis=-1, keepdims=True)
        - normed * jnp.mean(grad_normed * normed, axis=-1, keepdims=True)
    )


def product(spec, left, right):
    return jnp.einsum(spec, left, right, preferred_element_type=F32)


def add(left, right):
    return (left.astype(F32) + right.astype(F32)).astype(BF)


def finish_sum(parts, z_hi):
    mine = add(pick(parts, z_hi), moved(pick(parts, 1 - z_hi), z_hi=1, z_lo=1))
    mine = add(mine, moved(mine, z_lo=1))
    return gathered(mine, 1)


def core_sum(mine, send):
    return add(mine, moved(send, core=1))


def along_x(units):
    return total(exchanged(units.reshape(4, 2, *units.shape[1:]), 0)).astype(BF)


def along_y(quarters, y):
    mine = pick(quarters, y).astype(F32)
    for d in (1, 3, 2):
        mine = mine + moved(pick(quarters, (y + d) % 4), y=d).astype(F32)
    return mine.astype(BF)


def finish_kernel(owned, w_qkv, w_out, w_up, w_down, vectors):
    rows = [owned[q].astype(F32) for q in range(4)]
    gap = jnp.zeros((48, 512), F32)
    for i in range(3):
        columns = jnp.zeros((48, 768), F32)
        for q in range(4):
            part = jnp.concatenate([rows[q][:48, 256 * i : 256 * (i + 1)], gap], axis=1)
            columns = columns + (pltpu.roll(part, 192 * q, 1) if q else part)
        w_qkv[:, 768 * i : 768 * (i + 1)] = columns
    early = jnp.concatenate([part[64:] for part in rows], axis=0)
    w_out[...] = early[0:48]
    for i in range(4):
        w_up[:, 768 * i : 768 * (i + 1)] = early[48 + 48 * i : 96 + 48 * i]
    w_down[...] = early[256:448]
    vectors[...] = rows[0][48:64] + rows[1][48:64] + rows[2][48:64] + rows[3][48:64]


def finished(owned):
    shapes = [(48, 2304), (48, 768), (48, 3072), (192, 768), (16, 768)]
    return pl.pallas_call(
        finish_kernel,
        out_shape=[jax.ShapeDtypeStruct(shape, F32) for shape in shapes],
        name="finish_gradients",
    )(owned)


def local(
    tokens,
    lengths,
    cotangent,
    w_qkv,
    b_query,
    b_value,
    w_out,
    b_out,
    gain_one,
    shift_one,
    w_up,
    b_up,
    w_down,
    b_down,
    gain_two,
    shift_two,
):
    ctx, shard = lax.axis_index("ctx"), lax.axis_index("shard")
    y, z_lo = ctx // 2, ctx % 2
    x, z_hi, core = shard // 4, (shard // 2) % 2, shard % 2
    width = 768
    x_low = tokens[0]

    x_pair = jnp.stack([x_low, moved(x_low, z_lo=1)])
    x_pairs = [x_pair] + [moved(x_pair, y=d) for d in (1, 2, 3)]

    coords = jnp.stack([x, y, z_hi, core]).astype(jnp.int32)
    vectors = jnp.stack([b_query, b_value, b_out, gain_one, shift_one, b_down, gain_two, shift_two])
    vectors = jnp.concatenate([vectors, b_up.reshape(4, 48)], axis=0)
    vectors = jnp.pad(vectors, [(0, 4), (0, 80)])
    heads_own, w_out = lax.optimization_barrier((packed(coords, w_qkv, vectors), w_out))
    w_heads = lax.all_gather(heads_own, "shard", axis=0, tiled=True)
    rest_own = joined(w_out, w_up, w_down)
    rest_other = moved(rest_own, z_hi=1, z_lo=1)
    rest = gathered(rest_own, 0)
    x_pairs, rest, rest_other = lax.optimization_barrier((x_pairs, rest, rest_other))
    rest_far = gathered(rest_other, 0)

    near, far, narrow, b_up = project(coords, w_heads, x_pairs)
    length = lengths[0]
    block_of = [((y - c) % 4) * 2 + (z_lo if c < 4 else 1 - z_lo) for c in range(8)]
    limits = jnp.stack([length - 256 * block for block in block_of]).astype(jnp.int32)
    *out_low, out_full, log_total = forward_attention(limits, near, far)
    _, rest, rest_far = lax.optimization_barrier((out_low[0], rest, rest_far))

    def in_order(parts):
        blocks = jnp.stack(parts + parts)
        return lax.dynamic_slice_in_dim(blocks, (4 - y) % 4, 4, 0)

    attended = in_order([out_low[0]] + [moved(out_low[d], y=4 - d) for d in (1, 2, 3)])
    attended = attended.reshape(width, 256)

    w_out, up_all, w_down = unpacked(
        coords, rest, rest_far, moved(rest, core=1), moved(rest_far, core=1)
    )
    b_out, gain_one, shift_one, b_down, gain_two, shift_two = (narrow[i] for i in range(6))
    resid_one = x_low.astype(F32) + product("kt,kd->td", attended, w_out) + b_out
    hidden, normed_one, inverse_one = layer_norm(resid_one, gain_one, shift_one)
    hidden_low = hidden.astype(BF)
    upward = product("td,df->tf", hidden_low, up_all) + b_up
    active_low = gelu_value(upward).astype(BF)
    resid_two = hidden + product("tf,fd->td", active_low, w_down) + b_down
    mixed, normed_two, inverse_two = layer_norm(resid_two, gain_two, shift_two)
    grad_mixed = cotangent[0].astype(F32)
    grad_gain_two = jnp.sum(grad_mixed * normed_two, axis=0)
    grad_shift_two = jnp.sum(grad_mixed, axis=0)
    grad_resid_two = norm_back(grad_mixed, normed_two, inverse_two, gain_two)
    grad_down_low = grad_resid_two.astype(BF)
    grad_b_down = jnp.sum(grad_resid_two, axis=0)
    down_split = split_gradients(
        down_kernel,
        "down_gradients",
        192,
        4,
        [pltpu.SemaphoreType.DMA((2,)), pltpu.VMEM((256, 3072), BF), pltpu.VMEM((256, 768), BF)],
        coords,
        active_low,
        grad_down_low,
    )
    down_units = core_sum(*down_split)
    grad_upward = product("td,fd->tf", grad_down_low, w_down) * gelu_slope(upward)
    grad_up_low = grad_upward.astype(BF)
    grad_b_up = jnp.sum(grad_upward, axis=0)
    grad_hidden = grad_resid_two + product("tf,df->td", grad_up_low, up_all)
    grad_gain_one = jnp.sum(grad_hidden * normed_one, axis=0)
    grad_shift_one = jnp.sum(grad_hidden, axis=0)
    grad_resid_one = norm_back(grad_hidden, normed_one, inverse_one, gain_one)
    grad_out_low = grad_resid_one.astype(BF)
    grad_b_out = jnp.sum(grad_resid_one, axis=0)
    grad_out_low, down_units = lax.optimization_barrier((grad_out_low, down_units))
    grad_attended = product("kd,td->kt", w_out, grad_out_low).astype(BF).reshape(4, GROUP, HD, 256)

    grads = [pick(grad_attended, y)]
    for d in (1, 2, 3):
        grads.append(moved(pick(grad_attended, (y + d) % 4), y=d))
    grad_narrow = jnp.stack(
        [grad_b_out, grad_gain_one, grad_shift_one, grad_b_down, grad_gain_two, grad_shift_two]
    )
    up_split = list(split_gradients(
        up_kernel,
        "up_gradients",
        256,
        5,
        [
            pltpu.SemaphoreType.DMA((4,)),
            pltpu.VMEM((768, 256), BF),
            pltpu.VMEM((256, 768), BF),
            pltpu.VMEM((256, 768), BF),
            pltpu.VMEM((256, 3072), BF),
        ],
        coords,
        attended,
        hidden_low,
        grad_out_low,
        grad_up_low,
    ))

    down_raw = exchanged(down_units.reshape(4, 2, 192, width), 0)
    up_units = core_sum(*up_split)
    grads, up_units = lax.optimization_barrier((grads, up_units))
    grad_msgs = list(backward_attention(limits, near, far, grads, out_full, log_total))
    up_units, down_raw, grad_msgs[0] = lax.optimization_barrier((up_units, down_raw, grad_msgs[0]))
    up_own = along_x(up_units)

    mine, send, back = late_gradients(
        coords, w_heads, x_pairs, grad_msgs, grad_narrow, grad_b_up[None]
    )
    late_units, up_own = lax.optimization_barrier((core_sum(mine, send), up_own))
    late = along_x(late_units)
    arrived = [moved(back[d], y=4 - d) for d in (1, 2, 3)]
    arrived, up_own = lax.optimization_barrier((arrived, up_own))
    grad_pair = back[0].astype(F32)
    for part in arrived:
        grad_pair = grad_pair + part.astype(F32)
    from_other = moved(grad_pair[1].astype(BF), z_lo=1)
    down_own = total(down_raw).astype(BF)
    early = jnp.concatenate([up_own, down_own], axis=1).reshape(2, 4, 112, width)
    early = along_y(early.transpose(1, 0, 2, 3), y)
    owned = finish_sum(jnp.concatenate([late, early], axis=1), z_hi)
    grad_w_qkv, grad_w_out, grad_w_up, grad_w_down, vectors = finished(owned)
    grad_tokens = grad_resid_one + grad_pair[0] + from_other.astype(F32)

    def early_vector(first, count=48):
        return vectors[8, first : first + count]

    return (
        mixed.astype(BF)[None],
        grad_tokens[None],
        grad_w_qkv,
        vectors[0, 0:48],
        vectors[0, 48:96],
        grad_w_out,
        early_vector(0),
        early_vector(48),
        early_vector(96),
        grad_w_up,
        early_vector(288, 192),
        grad_w_down,
        early_vector(144),
        early_vector(192),
        early_vector(240),
    )


def solution(mesh):
    rows, vector = P("shard", None), P("shard")
    tokens = P("shard", "ctx", None)
    return jax.shard_map(
        local,
        mesh=mesh,
        in_specs=(
            tokens, vector, tokens, rows, vector, vector, rows, vector, vector, vector,
            rows, vector, rows, vector, vector, vector,
        ),
        out_specs=(
            tokens, tokens, rows, vector, vector, rows, vector, vector, vector, rows,
            vector, rows, vector, vector, vector,
        ),
        check_vma=False,
    )
```

```python
import jax
import jax.numpy as jnp
from jax import lax
from jax.experimental import pallas as pl
from jax.experimental.pallas import tpu as pltpu
from jax.sharding import PartitionSpec as P

H = 12
HD = 64
GROUP = 3
CTX = 8
SHARD = 16
AXES = ("ctx", "shard")
EPS = 1e-12
NEG = -1e30
SCALE = HD ** (-0.5)
BF = jnp.bfloat16
F32 = jnp.float32


def place(device):
    ctx, shard = divmod(device, SHARD)
    return [shard // 4, ctx // 2, (shard // 2) % 2, ctx % 2, shard % 2]


def device_at(x, y, z_hi, z_lo, core):
    return (y * 2 + z_lo) * SHARD + x * 4 + z_hi * 2 + core


def moved(value, x=0, y=0, z_hi=0, z_lo=0, core=0):
    pairs = []
    for source in range(CTX * SHARD):
        a, b, c, d, e = place(source)
        target = device_at((a + x) % 4, (b + y) % 4, (c + z_hi) % 2, (d + z_lo) % 2, (e + core) % 2)
        pairs.append((source, target))
    return lax.ppermute(value, AXES, pairs)


def groups_along(*axes):
    found = {}
    for device in range(CTX * SHARD):
        at = place(device)
        key = tuple(v for i, v in enumerate(at) if i not in axes)
        found.setdefault(key, []).append((tuple(at[i] for i in axes), device))
    return [[d for _, d in sorted(members)] for members in found.values()]


def exchanged(blocks, *axes):
    return lax.all_to_all(blocks, AXES, 0, 0, axis_index_groups=groups_along(*axes))


def gathered(block, *axes):
    count = len(groups_along(*axes)[0])
    return exchanged(jnp.broadcast_to(block[None], (count, *block.shape)), *axes)


def total(blocks, dim=0):
    return jnp.sum(blocks.astype(F32), axis=dim)


def pick(blocks, index, dim=0):
    return lax.dynamic_index_in_dim(blocks, index, dim, keepdims=False)


def brought(pairs, sems):
    copies = [pltpu.make_async_copy(source, to, sems.at[i]) for i, (source, to) in enumerate(pairs)]
    for copy in copies:
        copy.start()
    for copy in copies:
        copy.wait()


def with_rows(block, rows):
    at = lax.broadcasted_iota(jnp.int32, (16, block.shape[1]), 0)
    extra = jnp.zeros((16, block.shape[1]), F32)
    for place_, row in enumerate(rows):
        extra = jnp.where(at == place_, row, extra)
    rest = jnp.zeros((48, block.shape[1]), BF)
    return jnp.concatenate([block, extra.astype(BF), rest], axis=0)


def turned(block):
    return block.astype(F32).T.astype(BF)


def live_row(limit):
    tokens = lax.broadcasted_iota(jnp.int32, (1, 256), 1)
    return jnp.where(tokens < limit, 0.0, NEG)


def forward_kernel(limits, *refs):
    out_low, out_full, log_total = refs[8:12], refs[12], refs[13]
    key_scr, value_scr, near_scr, far_scr, sems = refs[14:19]
    h = pl.program_id(0)

    @pl.when(h == 0)
    def _():
        pairs = [(refs[d], near_scr.at[d]) for d in range(4)]
        brought(pairs + [(refs[4 + d], far_scr.at[d]) for d in range(4)], sems)

    ones = jnp.ones((1, 256), F32)
    for c in range(8):
        keys = near_scr[c, 1, h] if c < 4 else far_scr[c - 4, 0, h]
        values = near_scr[c, 2, h] if c < 4 else far_scr[c - 4, 1, h]
        key_scr[c] = turned(with_rows(keys, [live_row(limits[c])]))
        value_scr[c] = with_rows(values, [ones])[:80]
    for b in range(4):
        queries = with_rows((near_scr[b, 0, h].astype(F32) * SCALE).astype(BF), [ones])
        scores = [
            jnp.dot(key_scr[c], queries, preferred_element_type=F32) for c in range(8)
        ]
        top = scores[0]
        for c in range(1, 8):
            top = jnp.maximum(top, scores[c])
        row_max = jnp.max(top, axis=0, keepdims=True)
        out = jnp.zeros((80, 256), F32)
        for c in range(8):
            weights = jnp.exp(scores[c] - row_max).astype(BF)
            out = out + jnp.dot(value_scr[c], weights, preferred_element_type=F32)
        row_total = out[64:65]
        attended = out[:64] / row_total
        out_low[b][0] = attended.astype(BF)
        out_full[0, b] = attended
        log_total[0, b : b + 1] = row_max + jnp.log(row_total)


ARRIVED = [
    pltpu.VMEM((4, 3, GROUP, HD, 256), BF),
    pltpu.VMEM((4, 2, GROUP, HD, 256), BF),
    pltpu.SemaphoreType.DMA((14,)),
]


def forward_attention(limits, near, far):
    return pl.pallas_call(
        forward_kernel,
        grid=(GROUP,),
        in_specs=[pl.BlockSpec(memory_space=pltpu.SMEM)] + [pl.BlockSpec(memory_space=pltpu.HBM)] * 8,
        out_specs=[pl.BlockSpec((1, HD, 256), lambda h: (h, 0, 0))] * 4
        + [
            pl.BlockSpec((1, 4, HD, 256), lambda h: (h, 0, 0, 0)),
            pl.BlockSpec((1, 4, 256), lambda h: (h, 0, 0)),
        ],
        out_shape=[jax.ShapeDtypeStruct((GROUP, HD, 256), BF)] * 4
        + [
            jax.ShapeDtypeStruct((GROUP, 4, HD, 256), F32),
            jax.ShapeDtypeStruct((GROUP, 4, 256), F32),
        ],
        scratch_shapes=[pltpu.VMEM((8, 256, 128), BF), pltpu.VMEM((8, 80, 256), BF)] + ARRIVED,
        compiler_params=pltpu.CompilerParams(vmem_limit_bytes=60 * 2**20),
        cost_estimate=pl.CostEstimate(
            flops=12 * 2048 * 256 * 512, bytes_accessed=6 * 2**20, transcendentals=12 * 2048 * 256
        ),
        name="attention_forward",
    )(limits, *near, *far)


def split_rows(row, count):
    parts = []
    for _ in range(count):
        part = row.astype(BF).astype(F32)
        parts.append(part)
        row = row - part
    return parts


def backward_kernel(limits, *refs):
    grad_near, grad_far = refs[14:18], refs[18:22]
    query_scr, query_turned, grad_scr, grad_turned = refs[22:26]
    near_scr, far_scr, sems, grads_in, out_full, log_total = refs[26:32]
    h = pl.program_id(0)

    @pl.when(h == 0)
    def _():
        pairs = [(refs[d], near_scr.at[d]) for d in range(4)]
        pairs += [(refs[4 + d], far_scr.at[d]) for d in range(4)]
        pairs += [(refs[8 + d], grads_in.at[d]) for d in range(4)]
        brought(pairs + [(refs[12], out_full), (refs[13], log_total)], sems)

    ones = jnp.ones((1, 256), F32)
    for b in range(4):
        at = slice(256 * b, 256 * b + 256)
        log_rows = split_rows(-log_total[h, b : b + 1], 3)
        queries = with_rows((near_scr[b, 0, h].astype(F32) * SCALE).astype(BF), [ones] + log_rows)
        query_scr[:, at] = queries
        query_turned[at, :] = turned(queries)
        delta = jnp.sum(grads_in[b, h].astype(F32) * out_full[h, b], axis=0, keepdims=True)
        grad = with_rows(grads_in[b, h], split_rows(-delta, 2))
        grad_scr[:, at] = grad
        grad_turned[at, :] = turned(grad)
    grad_queries = jnp.zeros((HD, 1024), F32)
    for c in range(8):
        keys = near_scr[c, 1, h] if c < 4 else far_scr[c - 4, 0, h]
        values = near_scr[c, 2, h] if c < 4 else far_scr[c - 4, 1, h]
        key_rows = turned(with_rows(keys, [live_row(limits[c]), ones, ones, ones]))
        value_rows = turned(with_rows(values, [ones, ones]))
        weights = jnp.exp(jnp.dot(key_rows, query_scr[...], preferred_element_type=F32))
        grad_soft = jnp.dot(value_rows, grad_scr[...], preferred_element_type=F32)
        grad_scores = (weights * grad_soft).astype(BF)
        grad_values = jnp.dot(weights.astype(BF), grad_turned[...], preferred_element_type=F32)
        grad_keys = jnp.dot(grad_scores, query_turned[...], preferred_element_type=F32)
        grad_queries = grad_queries + jnp.dot(keys, grad_scores, preferred_element_type=F32)
        to, first = (grad_near[c], 1) if c < 4 else (grad_far[c - 4], 0)
        to[first, 0] = grad_keys.T[:HD].astype(BF)
        to[first + 1, 0] = grad_values.T[:HD].astype(BF)
    for b in range(4):
        grad_near[b][0, 0] = (grad_queries[:, 256 * b : 256 * b + 256] * SCALE).astype(BF)


def backward_attention(limits, near, far, grads, out_full, log_total):
    head = lambda h: (0, h, 0, 0)
    near_spec = pl.BlockSpec((3, 1, HD, 256), head)
    far_spec = pl.BlockSpec((2, 1, HD, 256), head)
    return pl.pallas_call(
        backward_kernel,
        grid=(GROUP,),
        in_specs=[pl.BlockSpec(memory_space=pltpu.SMEM)] + [pl.BlockSpec(memory_space=pltpu.HBM)] * 14,
        out_specs=[near_spec] * 4 + [far_spec] * 4,
        out_shape=[jax.ShapeDtypeStruct((3, GROUP, HD, 256), BF)] * 4
        + [jax.ShapeDtypeStruct((2, GROUP, HD, 256), BF)] * 4,
        scratch_shapes=[
            pltpu.VMEM((128, 1024), BF),
            pltpu.VMEM((1024, 128), BF),
            pltpu.VMEM((128, 1024), BF),
            pltpu.VMEM((1024, 128), BF),
        ]
        + ARRIVED
        + [
            pltpu.VMEM((4, GROUP, HD, 256), BF),
            pltpu.VMEM((GROUP, 4, HD, 256), F32),
            pltpu.VMEM((GROUP, 4, 256), F32),
        ],
        compiler_params=pltpu.CompilerParams(vmem_limit_bytes=60 * 2**20),
        cost_estimate=pl.CostEstimate(
            flops=12 * 2048 * 256 * 1280, bytes_accessed=12 * 2**20, transcendentals=12 * 2048 * 256
        ),
        name="attention_backward",
    )(limits, *near, *far, *grads, out_full, log_total)


def select(index, choices):
    result = choices[0]
    for i, choice in enumerate(choices[1:], 1):
        result = jnp.where(index == i, choice, result)
    return result


def pack_kernel(coords, w_qkv, vectors, qkv_out):
    whole = w_qkv[...].astype(F32)
    for i in range(3):
        choices = [whole[:, 768 * i + 192 * j : 768 * i + 192 * (j + 1)] for j in range(4)]
        part = jnp.concatenate([select(coords[1], choices), jnp.zeros((48, 64), F32)], axis=1)
        qkv_out[:, 256 * i : 256 * (i + 1)] = part.astype(BF)
    qkv_out[0:16, 768:] = vectors[...]
    qkv_out[16:48, 768:] = jnp.zeros((32, 128), BF)


def packed(coords, w_qkv, vectors):
    return pl.pallas_call(
        pack_kernel,
        in_specs=[pl.BlockSpec(memory_space=pltpu.SMEM)] + [pl.BlockSpec(memory_space=pltpu.VMEM)] * 2,
        out_shape=jax.ShapeDtypeStruct((48, 896), BF),
        name="pack_heads",
    )(coords, w_qkv, vectors)


def join_kernel(w_out, w_up, w_down, out):
    out[0:48] = w_out[...]
    for i in range(4):
        out[48 + 48 * i : 96 + 48 * i] = w_up[:, 768 * i : 768 * (i + 1)]
    out[240:432] = w_down[...]


def joined(w_out, w_up, w_down):
    return pl.pallas_call(
        join_kernel, out_shape=jax.ShapeDtypeStruct((432, 768), BF), name="join_parameters"
    )(w_out, w_up, w_down)


def spread(vectors, row, into, at):
    wide = into.shape[1]
    lanes = lax.broadcasted_iota(jnp.int32, (8, wide), 1)
    result = jnp.broadcast_to(into, (8, wide))
    for s in range(16):
        values = jnp.broadcast_to(vectors[s][row : row + 1], (8, 128))
        values = jnp.concatenate([values, jnp.zeros((8, wide - 128), F32)], axis=1)
        first = at(s)
        if first:
            values = pltpu.roll(values, first, 1)
        result = jnp.where(jnp.logical_and(lanes >= first, lanes < first + 48), values, result)
    return result[0:1]


def project_kernel(coords, *refs):
    near, far, narrow, wide = refs[5:9], refs[9:13], refs[13], refs[14]
    weights, x_all, vec_scr, sems = refs[15:19]
    brought([(refs[0], weights)] + [(refs[1 + d], x_all.at[d]) for d in range(4)], sems)
    for s in range(16):
        vec_scr[s] = weights[48 * s : 48 * s + 16, 768:].astype(F32)
    nothing = jnp.zeros((1, 768), F32)
    biases = []
    for i in range(2):
        row = jnp.broadcast_to(spread(vec_scr, i, nothing, lambda s: 48 * s), (8, 768))
        turns = [pltpu.roll(row, (768 - 192 * j) % 768, 1) if j else row for j in range(4)]
        biases.append(select(coords[1], turns)[0:1, :256])
    bias = jnp.concatenate([biases[0], jnp.zeros((1, 256), F32), biases[1]], axis=1)
    for c in range(8):
        if c < 4:
            part = jnp.dot(x_all[c, 0], weights[:, :768], preferred_element_type=F32) + bias
        else:
            part = jnp.dot(x_all[c - 4, 1], weights[:, 256:768], preferred_element_type=F32)
            part = part + bias[:, 256:]
        part = part.T.astype(BF)
        to = near[c] if c < 4 else far[c - 4]
        for i in range(3 if c < 4 else 2):
            for h in range(GROUP):
                at = 256 * i + 64 * h
                to[i, h] = part[at : at + 64]
    for i in range(6):
        narrow[i : i + 1] = spread(vec_scr, 2 + i, nothing, lambda s: 48 * s)
    up_row = jnp.zeros((1, 3072), F32)
    for i in range(4):
        up_row = spread(vec_scr, 8 + i, up_row, lambda s: 192 * s + 48 * i)
    wide[...] = up_row


def project(coords, w_heads, x_pairs):
    outs = pl.pallas_call(
        project_kernel,
        in_specs=[pl.BlockSpec(memory_space=pltpu.SMEM)] + [pl.BlockSpec(memory_space=pltpu.HBM)] * 5,
        out_shape=[jax.ShapeDtypeStruct((3, GROUP, HD, 256), BF)] * 4
        + [jax.ShapeDtypeStruct((2, GROUP, HD, 256), BF)] * 4
        + [jax.ShapeDtypeStruct((6, 768), F32), jax.ShapeDtypeStruct((1, 3072), F32)],
        scratch_shapes=[
            pltpu.VMEM((768, 896), BF),
            pltpu.VMEM((4, 2, 256, 768), BF),
            pltpu.VMEM((16, 16, 128), F32),
            pltpu.SemaphoreType.DMA((9,)),
        ],
        compiler_params=pltpu.CompilerParams(vmem_limit_bytes=60 * 2**20),
        cost_estimate=pl.CostEstimate(
            flops=2 * 2048 * 768 * 640, bytes_accessed=8 * 2**20, transcendentals=0
        ),
        name="project",
    )(coords, w_heads, *x_pairs)
    return outs[0:4], outs[4:8], outs[8], outs[9]


def unpack_kernel(coords, *refs):
    w_out, w_up, w_down = refs[4:7]
    for i, rest in enumerate(refs[0:4]):
        member = ((coords[2] + i % 2) % 2) * 2 + (coords[3] + i // 2) % 2
        rows = pl.ds(pl.multiple_of(member * 48, 16), 48)
        w_out[rows] = rest[0, 0:48]
        for i in range(4):
            w_up[rows, 768 * i : 768 * (i + 1)] = rest[0, 48 + 48 * i : 96 + 48 * i]
        w_down[pl.ds(pl.multiple_of(member * 192, 16), 192)] = rest[0, 240:432]


def unpacked(coords, *rests):
    block = pl.BlockSpec((1, 432, 768), lambda i: (i, 0, 0))
    return pl.pallas_call(
        unpack_kernel,
        grid=(4,),
        in_specs=[pl.BlockSpec(memory_space=pltpu.SMEM)] + [block] * 4,
        out_specs=[
            pl.BlockSpec((192, 768), lambda i: (i, 0)),
            pl.BlockSpec((192, 3072), lambda i: (i, 0)),
            pl.BlockSpec((768, 768), lambda i: (i, 0)),
        ],
        out_shape=[
            jax.ShapeDtypeStruct((768, 768), BF),
            jax.ShapeDtypeStruct((768, 3072), BF),
            jax.ShapeDtypeStruct((3072, 768), BF),
        ],
        compiler_params=pltpu.CompilerParams(vmem_limit_bytes=18 * 2**20),
        cost_estimate=pl.CostEstimate(flops=0, bytes_accessed=22 * 2**20, transcendentals=0),
        name="unpack_parameters",
    )(coords, *rests)


def collect(row, count, first, into):
    wide = row.shape[1]
    lanes = lax.broadcasted_iota(jnp.int32, (8, 768), 1)
    full = jnp.broadcast_to(row, (8, wide))
    inside = jnp.logical_and(lanes >= first, lanes < first + count)
    for s in range(16):
        shift = (first - s * count) % wide
        turned_row = pltpu.roll(full, shift, 1) if shift else full
        into[s] = jnp.where(inside, turned_row[:, :768], into[s])


def late_kernel(coords, *refs):
    narrow, wide, mine, send, back = refs[13], refs[14], refs[15], refs[16], refs[17:21]
    weights, x_all, near, far, sems, vec_scr = refs[21:27]
    y, first = coords[1], coords[3] == 0
    pairs = [(refs[0], weights)] + [(refs[1 + d], x_all.at[d]) for d in range(4)]
    pairs += [(refs[5 + d], near.at[d]) for d in range(4)]
    brought(pairs + [(refs[9 + d], far.at[d]) for d in range(4)], sems)
    ones = jnp.ones((256, 128), BF)
    totals, sums = [None] * 3, [None] * 3
    for c in range(8):
        back_part = jnp.zeros((768, 256), F32)
        for i in range(3):
            if c >= 4 and i == 0:
                continue
            grad = near[c, i] if c < 4 else far[c - 4, i - 1]
            grad = grad.reshape(192, 256)
            part = jnp.dot(grad, x_all[c % 4, c // 4], preferred_element_type=F32)
            row = jnp.dot(grad, ones, preferred_element_type=F32)
            totals[i] = part if totals[i] is None else totals[i] + part
            sums[i] = row if sums[i] is None else sums[i] + row
            back_part = back_part + jnp.dot(
                weights[:, 256 * i : 256 * i + 192], grad, preferred_element_type=F32
            )
        back[c % 4][c // 4] = back_part.T.astype(BF)
    gap = jnp.zeros((64, 768), F32)
    grads = jnp.concatenate([jnp.concatenate([t, gap], axis=0).T for t in totals], axis=1)
    for u in range(8):
        store_split(first, mine, send, u, 0, 48, grads[96 * u : 96 * u + 96])
    rows = []
    for i in (0, 2):
        row = jnp.concatenate([sums[i], jnp.zeros((64, 128), F32)], axis=0).T[0:8]
        rows.append(jnp.concatenate([row, jnp.zeros((8, 512), F32)], axis=1))
    lanes = lax.broadcasted_iota(jnp.int32, (8, 768), 1)
    vectors = []
    for j in range(4):
        query = pltpu.roll(rows[0], (768 - 48 * j) % 768, 1) if j else rows[0]
        shift = (768 + 48 - 48 * j) % 768
        value = pltpu.roll(rows[1], shift, 1) if shift else rows[1]
        vector = jnp.where(lanes < 48, query, jnp.where(lanes < 96, value, 0.0))
        vectors.append(vector)
    vec_scr[...] = jnp.zeros((16, 8, 768), F32)
    for i in range(6):
        collect(narrow[i : i + 1], 48, 48 * i, vec_scr)
    collect(wide[...], 192, 288, vec_scr)
    nothing = jnp.zeros((8, 768), F32)
    for u in range(8):
        both = [nothing, vec_scr[2 * u], nothing, vec_scr[2 * u + 1]]
        store_split(first, mine, send, u, 48, 16, jnp.concatenate(both, axis=0))
    for j in range(2):
        unit = 2 * y + j
        both = [vectors[2 * j], vec_scr[2 * unit], vectors[2 * j + 1], vec_scr[2 * unit + 1]]
        store_split(first, mine, send, unit, 48, 16, jnp.concatenate(both, axis=0))


def late_gradients(coords, w_heads, x_pairs, grad_msgs, narrow, wide):
    outs = pl.pallas_call(
        late_kernel,
        in_specs=[pl.BlockSpec(memory_space=pltpu.SMEM)]
        + [pl.BlockSpec(memory_space=pltpu.HBM)] * 13
        + [pl.BlockSpec(memory_space=pltpu.VMEM)] * 2,
        out_shape=[jax.ShapeDtypeStruct((8, 64, 768), BF)] * 2
        + [jax.ShapeDtypeStruct((2, 256, 768), BF)] * 4,
        scratch_shapes=[
            pltpu.VMEM((768, 896), BF),
            pltpu.VMEM((4, 2, 256, 768), BF),
            pltpu.VMEM((4, 3, GROUP, HD, 256), BF),
            pltpu.VMEM((4, 2, GROUP, HD, 256), BF),
            pltpu.SemaphoreType.DMA((17,)),
            pltpu.VMEM((16, 8, 768), F32),
        ],
        compiler_params=pltpu.CompilerParams(vmem_limit_bytes=60 * 2**20),
        cost_estimate=pl.CostEstimate(
            flops=4 * 2048 * 768 * 512, bytes_accessed=12 * 2**20, transcendentals=0
        ),
        name="late_gradients",
    )(coords, w_heads, *x_pairs, *grad_msgs, narrow, wide)
    return outs[0], outs[1], outs[2:]


def store_split(first, mine, send, unit, at, height, rows):
    even, odd = rows[:height], rows[height:]
    mine[unit, at : at + height] = jnp.where(first, even, odd).astype(BF)
    send[unit, at : at + height] = jnp.where(first, odd, even).astype(BF)


def down_kernel(coords, active_in, grad_in, mine, send, sems, active, grad_down):
    brought([(active_in, active), (grad_in, grad_down)], sems)
    first = coords[3] == 0
    for i in range(4):
        weights = lax.dot_general(
            active[:, 768 * i : 768 * (i + 1)],
            grad_down[...],
            (((0,), (0,)), ((), ())),
            preferred_element_type=F32,
        )
        for u in range(2):
            store_split(first, mine, send, 2 * i + u, 0, 192, weights[384 * u : 384 * u + 384])


def up_kernel(coords, *refs):
    mine, send, sems = refs[4:7]
    brought(list(zip(refs[0:4], refs[7:11])), sems)
    attended, hidden, grad_out, grad_up = refs[7:11]
    first = coords[3] == 0
    hidden_turned = hidden[...].astype(F32).T.astype(BF)
    for i in range(4):
        weights = jnp.dot(
            hidden_turned, grad_up[:, 768 * i : 768 * (i + 1)], preferred_element_type=F32
        )
        for u in range(8):
            store_split(first, mine, send, u, 48 + 48 * i, 48, weights[96 * u : 96 * u + 96])
    weights = jnp.dot(attended[...], grad_out[...], preferred_element_type=F32)
    for u in range(8):
        store_split(first, mine, send, u, 0, 48, weights[96 * u : 96 * u + 96])
    for u in range(8):
        mine[u, 240:256] = jnp.zeros((16, 768), BF)
        send[u, 240:256] = jnp.zeros((16, 768), BF)


def split_gradients(kernel, name, rows, blocks, scratch, coords, *arrays):
    return pl.pallas_call(
        kernel,
        in_specs=[pl.BlockSpec(memory_space=pltpu.SMEM)]
        + [pl.BlockSpec(memory_space=pl.ANY)] * len(arrays),
        out_shape=[jax.ShapeDtypeStruct((8, rows, 768), BF)] * 2,
        scratch_shapes=scratch,
        compiler_params=pltpu.CompilerParams(vmem_limit_bytes=20 * 2**20),
        cost_estimate=pl.CostEstimate(
            flops=2 * 256 * 768 * 768 * blocks, bytes_accessed=2 * 2**20 * blocks, transcendentals=0
        ),
        name=name,
    )(coords, *arrays)


def gelu_value(upward):
    return 0.5 * upward * (1.0 + lax.erf(upward * 0.7071067811865476))


def gelu_slope(upward):
    return (
        0.5 * (1.0 + lax.erf(upward * 0.7071067811865476))
        + upward * jnp.exp(-0.5 * upward * upward) * 0.3989422804014327
    )


def layer_norm(resid, gain, shift):
    mean = jnp.mean(resid, axis=-1, keepdims=True)
    centered = resid - mean
    spread = jnp.mean(centered * centered, axis=-1, keepdims=True)
    inverse = lax.rsqrt(spread + EPS)
    normed = centered * inverse
    return (normed * gain + shift, normed, inverse)


def norm_back(grad_out, normed, inverse, gain):
    grad_normed = grad_out * gain
    return inverse * (
        grad_normed
        - jnp.mean(grad_normed, axis=-1, keepdims=True)
        - normed * jnp.mean(grad_normed * normed, axis=-1, keepdims=True)
    )


def product(spec, left, right):
    return jnp.einsum(spec, left, right, preferred_element_type=F32)


def add(left, right):
    return (left.astype(F32) + right.astype(F32)).astype(BF)


def finish_sum(parts, z_hi):
    mine = add(pick(parts, z_hi), moved(pick(parts, 1 - z_hi), z_hi=1, z_lo=1))
    mine = add(mine, moved(mine, z_lo=1))
    return gathered(mine, 1)


def core_sum(mine, send):
    return add(mine, moved(send, core=1))


def along_x(units):
    return total(exchanged(units.reshape(4, 2, *units.shape[1:]), 0)).astype(BF)


def along_y(quarters, y):
    mine = pick(quarters, y).astype(F32)
    for d in (1, 3, 2):
        mine = mine + moved(pick(quarters, (y + d) % 4), y=d).astype(F32)
    return mine.astype(BF)


def finish_kernel(owned, w_qkv, w_out, w_up, w_down, vectors):
    rows = [owned[q].astype(F32) for q in range(4)]
    gap = jnp.zeros((48, 512), F32)
    for i in range(3):
        columns = jnp.zeros((48, 768), F32)
        for q in range(4):
            part = jnp.concatenate([rows[q][:48, 256 * i : 256 * (i + 1)], gap], axis=1)
            columns = columns + (pltpu.roll(part, 192 * q, 1) if q else part)
        w_qkv[:, 768 * i : 768 * (i + 1)] = columns
    early = jnp.concatenate([part[64:] for part in rows], axis=0)
    w_out[...] = early[0:48]
    for i in range(4):
        w_up[:, 768 * i : 768 * (i + 1)] = early[48 + 48 * i : 96 + 48 * i]
    w_down[...] = early[256:448]
    vectors[...] = rows[0][48:64] + rows[1][48:64] + rows[2][48:64] + rows[3][48:64]


def finished(owned):
    shapes = [(48, 2304), (48, 768), (48, 3072), (192, 768), (16, 768)]
    return pl.pallas_call(
        finish_kernel,
        out_shape=[jax.ShapeDtypeStruct(shape, F32) for shape in shapes],
        name="finish_gradients",
    )(owned)


def local(
    tokens,
    lengths,
    cotangent,
    w_qkv,
    b_query,
    b_value,
    w_out,
    b_out,
    gain_one,
    shift_one,
    w_up,
    b_up,
    w_down,
    b_down,
    gain_two,
    shift_two,
):
    ctx, shard = lax.axis_index("ctx"), lax.axis_index("shard")
    y, z_lo = ctx // 2, ctx % 2
    x, z_hi, core = shard // 4, (shard // 2) % 2, shard % 2
    width = 768
    x_low = tokens[0]

    x_pair = jnp.stack([x_low, moved(x_low, z_lo=1)])
    x_pairs = [x_pair] + [moved(x_pair, y=d) for d in (1, 2, 3)]

    coords = jnp.stack([x, y, z_hi, core]).astype(jnp.int32)
    vectors = jnp.stack([b_query, b_value, b_out, gain_one, shift_one, b_down, gain_two, shift_two])
    vectors = jnp.concatenate([vectors, b_up.reshape(4, 48)], axis=0)
    vectors = jnp.pad(vectors, [(0, 4), (0, 80)])
    heads_own, w_out = lax.optimization_barrier((packed(coords, w_qkv, vectors), w_out))
    w_heads = lax.all_gather(heads_own, "shard", axis=0, tiled=True)
    rest_own = joined(w_out, w_up, w_down)
    rest_other = moved(rest_own, z_hi=1, z_lo=1)
    rest = gathered(rest_own, 0)
    x_pairs[1], x_pairs[3], rest, rest_other = lax.optimization_barrier(
        (x_pairs[1], x_pairs[3], rest, rest_other)
    )
    rest_far = gathered(rest_other, 0)

    near, far, narrow, b_up = project(coords, w_heads, x_pairs)
    length = lengths[0]
    block_of = [((y - c) % 4) * 2 + (z_lo if c < 4 else 1 - z_lo) for c in range(8)]
    limits = jnp.stack([length - 256 * block for block in block_of]).astype(jnp.int32)
    *out_low, out_full, log_total = forward_attention(limits, near, far)
    _, rest_far = lax.optimization_barrier((out_low[0], rest_far))

    def in_order(parts):
        blocks = jnp.stack(parts + parts)
        return lax.dynamic_slice_in_dim(blocks, (4 - y) % 4, 4, 0)

    attended = in_order([out_low[0]] + [moved(out_low[d], y=4 - d) for d in (1, 2, 3)])
    attended = attended.reshape(width, 256)

    w_out, up_all, w_down = unpacked(
        coords, rest, rest_far, moved(rest, core=1), moved(rest_far, core=1)
    )
    b_out, gain_one, shift_one, b_down, gain_two, shift_two = (narrow[i] for i in range(6))
    resid_one = x_low.astype(F32) + product("kt,kd->td", attended, w_out) + b_out
    hidden, normed_one, inverse_one = layer_norm(resid_one, gain_one, shift_one)
    hidden_low = hidden.astype(BF)
    upward = product("td,df->tf", hidden_low, up_all) + b_up
    active_low = gelu_value(upward).astype(BF)
    resid_two = hidden + product("tf,fd->td", active_low, w_down) + b_down
    mixed, normed_two, inverse_two = layer_norm(resid_two, gain_two, shift_two)
    grad_mixed = cotangent[0].astype(F32)
    grad_gain_two = jnp.sum(grad_mixed * normed_two, axis=0)
    grad_shift_two = jnp.sum(grad_mixed, axis=0)
    grad_resid_two = norm_back(grad_mixed, normed_two, inverse_two, gain_two)
    grad_down_low = grad_resid_two.astype(BF)
    grad_b_down = jnp.sum(grad_resid_two, axis=0)
    down_split = split_gradients(
        down_kernel,
        "down_gradients",
        192,
        4,
        [pltpu.SemaphoreType.DMA((2,)), pltpu.VMEM((256, 3072), BF), pltpu.VMEM((256, 768), BF)],
        coords,
        active_low,
        grad_down_low,
    )
    down_units = core_sum(*down_split)
    grad_upward = product("td,fd->tf", grad_down_low, w_down) * gelu_slope(upward)
    grad_up_low = grad_upward.astype(BF)
    grad_b_up = jnp.sum(grad_upward, axis=0)
    grad_hidden = grad_resid_two + product("tf,df->td", grad_up_low, up_all)
    grad_gain_one = jnp.sum(grad_hidden * normed_one, axis=0)
    grad_shift_one = jnp.sum(grad_hidden, axis=0)
    grad_resid_one = norm_back(grad_hidden, normed_one, inverse_one, gain_one)
    grad_out_low = grad_resid_one.astype(BF)
    grad_b_out = jnp.sum(grad_resid_one, axis=0)
    grad_out_low, down_units = lax.optimization_barrier((grad_out_low, down_units))
    grad_attended = product("kd,td->kt", w_out, grad_out_low).astype(BF).reshape(4, GROUP, HD, 256)

    grads = [pick(grad_attended, y)]
    for d in (1, 2, 3):
        grads.append(moved(pick(grad_attended, (y + d) % 4), y=d))
    grad_narrow = jnp.stack(
        [grad_b_out, grad_gain_one, grad_shift_one, grad_b_down, grad_gain_two, grad_shift_two]
    )
    up_split = list(split_gradients(
        up_kernel,
        "up_gradients",
        256,
        5,
        [
            pltpu.SemaphoreType.DMA((4,)),
            pltpu.VMEM((768, 256), BF),
            pltpu.VMEM((256, 768), BF),
            pltpu.VMEM((256, 768), BF),
            pltpu.VMEM((256, 3072), BF),
        ],
        coords,
        attended,
        hidden_low,
        grad_out_low,
        grad_up_low,
    ))

    down_raw = exchanged(down_units.reshape(4, 2, 192, width), 0)
    up_units = core_sum(*up_split)
    grads, up_units = lax.optimization_barrier((grads, up_units))
    grad_msgs = list(backward_attention(limits, near, far, grads, out_full, log_total))
    up_units, down_raw, grad_msgs[0] = lax.optimization_barrier((up_units, down_raw, grad_msgs[0]))
    up_own = along_x(up_units)

    mine, send, back = late_gradients(
        coords, w_heads, x_pairs, grad_msgs, grad_narrow, grad_b_up[None]
    )
    late_units, up_own = lax.optimization_barrier((core_sum(mine, send), up_own))
    late = along_x(late_units)
    arrived = [moved(back[d], y=4 - d) for d in (1, 2, 3)]
    arrived, up_own = lax.optimization_barrier((arrived, up_own))
    grad_pair = back[0].astype(F32)
    for part in arrived:
        grad_pair = grad_pair + part.astype(F32)
    from_other = moved(grad_pair[1].astype(BF), z_lo=1)
    down_own = total(down_raw).astype(BF)
    early = jnp.concatenate([up_own, down_own], axis=1).reshape(2, 4, 112, width)
    early = along_y(early.transpose(1, 0, 2, 3), y)
    owned = finish_sum(jnp.concatenate([late, early], axis=1), z_hi)
    grad_w_qkv, grad_w_out, grad_w_up, grad_w_down, vectors = finished(owned)
    grad_tokens = grad_resid_one + grad_pair[0] + from_other.astype(F32)

    def early_vector(first, count=48):
        return vectors[8, first : first + count]

    return (
        mixed.astype(BF)[None],
        grad_tokens[None],
        grad_w_qkv,
        vectors[0, 0:48],
        vectors[0, 48:96],
        grad_w_out,
        early_vector(0),
        early_vector(48),
        early_vector(96),
        grad_w_up,
        early_vector(288, 192),
        grad_w_down,
        early_vector(144),
        early_vector(192),
        early_vector(240),
    )


def solution(mesh):
    rows, vector = P("shard", None), P("shard")
    tokens = P("shard", "ctx", None)
    return jax.shard_map(
        local,
        mesh=mesh,
        in_specs=(
            tokens, vector, tokens, rows, vector, vector, rows, vector, vector, vector,
            rows, vector, rows, vector, vector, vector,
        ),
        out_specs=(
            tokens, tokens, rows, vector, vector, rows, vector, vector, vector, rows,
            vector, rows, vector, vector, vector,
        ),
        check_vma=False,
    )
```

```python
import jax
import jax.numpy as jnp
from jax import lax
from jax.experimental import pallas as pl
from jax.experimental.pallas import tpu as pltpu
from jax.sharding import PartitionSpec as P

H = 12
HD = 64
GROUP = 3
CTX = 8
SHARD = 16
AXES = ("ctx", "shard")
EPS = 1e-12
NEG = -1e30
SCALE = HD ** (-0.5)
BF = jnp.bfloat16
F32 = jnp.float32


def place(device):
    ctx, shard = divmod(device, SHARD)
    return [shard // 4, ctx // 2, (shard // 2) % 2, ctx % 2, shard % 2]


def device_at(x, y, z_hi, z_lo, core):
    return (y * 2 + z_lo) * SHARD + x * 4 + z_hi * 2 + core


def moved(value, x=0, y=0, z_hi=0, z_lo=0, core=0):
    pairs = []
    for source in range(CTX * SHARD):
        a, b, c, d, e = place(source)
        target = device_at((a + x) % 4, (b + y) % 4, (c + z_hi) % 2, (d + z_lo) % 2, (e + core) % 2)
        pairs.append((source, target))
    return lax.ppermute(value, AXES, pairs)


def groups_along(*axes):
    found = {}
    for device in range(CTX * SHARD):
        at = place(device)
        key = tuple(v for i, v in enumerate(at) if i not in axes)
        found.setdefault(key, []).append((tuple(at[i] for i in axes), device))
    return [[d for _, d in sorted(members)] for members in found.values()]


def exchanged(blocks, *axes):
    return lax.all_to_all(blocks, AXES, 0, 0, axis_index_groups=groups_along(*axes))


def gathered(block, *axes):
    count = len(groups_along(*axes)[0])
    return exchanged(jnp.broadcast_to(block[None], (count, *block.shape)), *axes)


def total(blocks, dim=0):
    return jnp.sum(blocks.astype(F32), axis=dim)


def pick(blocks, index, dim=0):
    return lax.dynamic_index_in_dim(blocks, index, dim, keepdims=False)


def brought(pairs, sems):
    copies = [pltpu.make_async_copy(source, to, sems.at[i]) for i, (source, to) in enumerate(pairs)]
    for copy in copies:
        copy.start()
    for copy in copies:
        copy.wait()


def with_rows(block, rows):
    at = lax.broadcasted_iota(jnp.int32, (16, block.shape[1]), 0)
    extra = jnp.zeros((16, block.shape[1]), F32)
    for place_, row in enumerate(rows):
        extra = jnp.where(at == place_, row, extra)
    rest = jnp.zeros((48, block.shape[1]), BF)
    return jnp.concatenate([block, extra.astype(BF), rest], axis=0)


def turned(block):
    return block.astype(F32).T.astype(BF)


def live_row(limit):
    tokens = lax.broadcasted_iota(jnp.int32, (1, 256), 1)
    return jnp.where(tokens < limit, 0.0, NEG)


def forward_kernel(limits, *refs):
    out_low, out_full, log_total = refs[8:12], refs[12], refs[13]
    key_scr, value_scr, near_scr, far_scr, sems = refs[14:19]
    h = pl.program_id(0)

    @pl.when(h == 0)
    def _():
        pairs = [(refs[d], near_scr.at[d]) for d in range(4)]
        brought(pairs + [(refs[4 + d], far_scr.at[d]) for d in range(4)], sems)

    ones = jnp.ones((1, 256), F32)
    for c in range(8):
        keys = near_scr[c, 1, h] if c < 4 else far_scr[c - 4, 0, h]
        values = near_scr[c, 2, h] if c < 4 else far_scr[c - 4, 1, h]
        key_scr[c] = turned(with_rows(keys, [live_row(limits[c])]))
        value_scr[c] = with_rows(values, [ones])[:80]
    for b in range(4):
        queries = with_rows((near_scr[b, 0, h].astype(F32) * SCALE).astype(BF), [ones])
        scores = [
            jnp.dot(key_scr[c], queries, preferred_element_type=F32) for c in range(8)
        ]
        top = scores[0]
        for c in range(1, 8):
            top = jnp.maximum(top, scores[c])
        row_max = jnp.max(top, axis=0, keepdims=True)
        out = jnp.zeros((80, 256), F32)
        for c in range(8):
            weights = jnp.exp(scores[c] - row_max).astype(BF)
            out = out + jnp.dot(value_scr[c], weights, preferred_element_type=F32)
        row_total = out[64:65]
        attended = out[:64] / row_total
        out_low[b][0] = attended.astype(BF)
        out_full[0, b] = attended
        log_total[0, b : b + 1] = row_max + jnp.log(row_total)


ARRIVED = [
    pltpu.VMEM((4, 3, GROUP, HD, 256), BF),
    pltpu.VMEM((4, 2, GROUP, HD, 256), BF),
    pltpu.SemaphoreType.DMA((14,)),
]


def forward_attention(limits, near, far):
    return pl.pallas_call(
        forward_kernel,
        grid=(GROUP,),
        in_specs=[pl.BlockSpec(memory_space=pltpu.SMEM)] + [pl.BlockSpec(memory_space=pltpu.HBM)] * 8,
        out_specs=[pl.BlockSpec((1, HD, 256), lambda h: (h, 0, 0))] * 4
        + [
            pl.BlockSpec((1, 4, HD, 256), lambda h: (h, 0, 0, 0)),
            pl.BlockSpec((1, 4, 256), lambda h: (h, 0, 0)),
        ],
        out_shape=[jax.ShapeDtypeStruct((GROUP, HD, 256), BF)] * 4
        + [
            jax.ShapeDtypeStruct((GROUP, 4, HD, 256), F32),
            jax.ShapeDtypeStruct((GROUP, 4, 256), F32),
        ],
        scratch_shapes=[pltpu.VMEM((8, 256, 128), BF), pltpu.VMEM((8, 80, 256), BF)] + ARRIVED,
        compiler_params=pltpu.CompilerParams(vmem_limit_bytes=60 * 2**20),
        cost_estimate=pl.CostEstimate(
            flops=12 * 2048 * 256 * 512, bytes_accessed=6 * 2**20, transcendentals=12 * 2048 * 256
        ),
        name="attention_forward",
    )(limits, *near, *far)


def split_rows(row, count):
    parts = []
    for _ in range(count):
        part = row.astype(BF).astype(F32)
        parts.append(part)
        row = row - part
    return parts


def backward_kernel(limits, *refs):
    grad_near, grad_far = refs[14:18], refs[18:22]
    query_scr, query_turned, grad_scr, grad_turned = refs[22:26]
    near_scr, far_scr, sems, grads_in, out_full, log_total = refs[26:32]
    h = pl.program_id(0)

    @pl.when(h == 0)
    def _():
        pairs = [(refs[d], near_scr.at[d]) for d in range(4)]
        pairs += [(refs[4 + d], far_scr.at[d]) for d in range(4)]
        pairs += [(refs[8 + d], grads_in.at[d]) for d in range(4)]
        brought(pairs + [(refs[12], out_full), (refs[13], log_total)], sems)

    ones = jnp.ones((1, 256), F32)
    for b in range(4):
        at = slice(256 * b, 256 * b + 256)
        log_rows = split_rows(-log_total[h, b : b + 1], 3)
        queries = with_rows((near_scr[b, 0, h].astype(F32) * SCALE).astype(BF), [ones] + log_rows)
        query_scr[:, at] = queries
        query_turned[at, :] = turned(queries)
        delta = jnp.sum(grads_in[b, h].astype(F32) * out_full[h, b], axis=0, keepdims=True)
        grad = with_rows(grads_in[b, h], split_rows(-delta, 2))
        grad_scr[:, at] = grad
        grad_turned[at, :] = turned(grad)
    grad_queries = jnp.zeros((HD, 1024), F32)
    for c in range(8):
        keys = near_scr[c, 1, h] if c < 4 else far_scr[c - 4, 0, h]
        values = near_scr[c, 2, h] if c < 4 else far_scr[c - 4, 1, h]
        key_rows = turned(with_rows(keys, [live_row(limits[c]), ones, ones, ones]))
        value_rows = turned(with_rows(values, [ones, ones]))
        weights = jnp.exp(jnp.dot(key_rows, query_scr[...], preferred_element_type=F32))
        grad_soft = jnp.dot(value_rows, grad_scr[...], preferred_element_type=F32)
        grad_scores = (weights * grad_soft).astype(BF)
        grad_values = jnp.dot(weights.astype(BF), grad_turned[...], preferred_element_type=F32)
        grad_keys = jnp.dot(grad_scores, query_turned[...], preferred_element_type=F32)
        grad_queries = grad_queries + jnp.dot(keys, grad_scores, preferred_element_type=F32)
        to, first = (grad_near[c], 1) if c < 4 else (grad_far[c - 4], 0)
        to[first, 0] = grad_keys.T[:HD].astype(BF)
        to[first + 1, 0] = grad_values.T[:HD].astype(BF)
    for b in range(4):
        grad_near[b][0, 0] = (grad_queries[:, 256 * b : 256 * b + 256] * SCALE).astype(BF)


def backward_attention(limits, near, far, grads, out_full, log_total):
    head = lambda h: (0, h, 0, 0)
    near_spec = pl.BlockSpec((3, 1, HD, 256), head)
    far_spec = pl.BlockSpec((2, 1, HD, 256), head)
    return pl.pallas_call(
        backward_kernel,
        grid=(GROUP,),
        in_specs=[pl.BlockSpec(memory_space=pltpu.SMEM)] + [pl.BlockSpec(memory_space=pltpu.HBM)] * 14,
        out_specs=[near_spec] * 4 + [far_spec] * 4,
        out_shape=[jax.ShapeDtypeStruct((3, GROUP, HD, 256), BF)] * 4
        + [jax.ShapeDtypeStruct((2, GROUP, HD, 256), BF)] * 4,
        scratch_shapes=[
            pltpu.VMEM((128, 1024), BF),
            pltpu.VMEM((1024, 128), BF),
            pltpu.VMEM((128, 1024), BF),
            pltpu.VMEM((1024, 128), BF),
        ]
        + ARRIVED
        + [
            pltpu.VMEM((4, GROUP, HD, 256), BF),
            pltpu.VMEM((GROUP, 4, HD, 256), F32),
            pltpu.VMEM((GROUP, 4, 256), F32),
        ],
        compiler_params=pltpu.CompilerParams(vmem_limit_bytes=60 * 2**20),
        cost_estimate=pl.CostEstimate(
            flops=12 * 2048 * 256 * 1280, bytes_accessed=12 * 2**20, transcendentals=12 * 2048 * 256
        ),
        name="attention_backward",
    )(limits, *near, *far, *grads, out_full, log_total)


def select(index, choices):
    result = choices[0]
    for i, choice in enumerate(choices[1:], 1):
        result = jnp.where(index == i, choice, result)
    return result


def pack_kernel(coords, w_qkv, vectors, qkv_out):
    whole = w_qkv[...].astype(F32)
    for i in range(3):
        choices = [whole[:, 768 * i + 192 * j : 768 * i + 192 * (j + 1)] for j in range(4)]
        part = jnp.concatenate([select(coords[1], choices), jnp.zeros((48, 64), F32)], axis=1)
        qkv_out[:, 256 * i : 256 * (i + 1)] = part.astype(BF)
    qkv_out[0:16, 768:] = vectors[...]
    qkv_out[16:48, 768:] = jnp.zeros((32, 128), BF)


def packed(coords, w_qkv, vectors):
    return pl.pallas_call(
        pack_kernel,
        in_specs=[pl.BlockSpec(memory_space=pltpu.SMEM)] + [pl.BlockSpec(memory_space=pltpu.VMEM)] * 2,
        out_shape=jax.ShapeDtypeStruct((48, 896), BF),
        name="pack_heads",
    )(coords, w_qkv, vectors)


def join_kernel(w_out, w_up, w_down, out):
    out[0:48] = w_out[...]
    for i in range(4):
        out[48 + 48 * i : 96 + 48 * i] = w_up[:, 768 * i : 768 * (i + 1)]
    out[240:432] = w_down[...]


def joined(w_out, w_up, w_down):
    return pl.pallas_call(
        join_kernel, out_shape=jax.ShapeDtypeStruct((432, 768), BF), name="join_parameters"
    )(w_out, w_up, w_down)


def spread(vectors, row, into, at):
    wide = into.shape[1]
    lanes = lax.broadcasted_iota(jnp.int32, (8, wide), 1)
    result = jnp.broadcast_to(into, (8, wide))
    for s in range(16):
        values = jnp.broadcast_to(vectors[s][row : row + 1], (8, 128))
        values = jnp.concatenate([values, jnp.zeros((8, wide - 128), F32)], axis=1)
        first = at(s)
        if first:
            values = pltpu.roll(values, first, 1)
        result = jnp.where(jnp.logical_and(lanes >= first, lanes < first + 48), values, result)
    return result[0:1]


def project_kernel(coords, *refs):
    near, far, narrow, wide = refs[5:9], refs[9:13], refs[13], refs[14]
    weights, x_all, vec_scr, sems = refs[15:19]
    brought([(refs[0], weights)] + [(refs[1 + d], x_all.at[d]) for d in range(4)], sems)
    for s in range(16):
        vec_scr[s] = weights[48 * s : 48 * s + 16, 768:].astype(F32)
    nothing = jnp.zeros((1, 768), F32)
    biases = []
    for i in range(2):
        row = jnp.broadcast_to(spread(vec_scr, i, nothing, lambda s: 48 * s), (8, 768))
        turns = [pltpu.roll(row, (768 - 192 * j) % 768, 1) if j else row for j in range(4)]
        biases.append(select(coords[1], turns)[0:1, :256])
    bias = jnp.concatenate([biases[0], jnp.zeros((1, 256), F32), biases[1]], axis=1)
    for c in range(8):
        if c < 4:
            part = jnp.dot(x_all[c, 0], weights[:, :768], preferred_element_type=F32) + bias
        else:
            part = jnp.dot(x_all[c - 4, 1], weights[:, 256:768], preferred_element_type=F32)
            part = part + bias[:, 256:]
        part = part.T.astype(BF)
        to = near[c] if c < 4 else far[c - 4]
        for i in range(3 if c < 4 else 2):
            for h in range(GROUP):
                at = 256 * i + 64 * h
                to[i, h] = part[at : at + 64]
    for i in range(6):
        narrow[i : i + 1] = spread(vec_scr, 2 + i, nothing, lambda s: 48 * s)
    up_row = jnp.zeros((1, 3072), F32)
    for i in range(4):
        up_row = spread(vec_scr, 8 + i, up_row, lambda s: 192 * s + 48 * i)
    wide[...] = up_row


def project(coords, w_heads, x_pairs):
    outs = pl.pallas_call(
        project_kernel,
        in_specs=[pl.BlockSpec(memory_space=pltpu.SMEM)] + [pl.BlockSpec(memory_space=pltpu.HBM)] * 5,
        out_shape=[jax.ShapeDtypeStruct((3, GROUP, HD, 256), BF)] * 4
        + [jax.ShapeDtypeStruct((2, GROUP, HD, 256), BF)] * 4
        + [jax.ShapeDtypeStruct((6, 768), F32), jax.ShapeDtypeStruct((1, 3072), F32)],
        scratch_shapes=[
            pltpu.VMEM((768, 896), BF),
            pltpu.VMEM((4, 2, 256, 768), BF),
            pltpu.VMEM((16, 16, 128), F32),
            pltpu.SemaphoreType.DMA((9,)),
        ],
        compiler_params=pltpu.CompilerParams(vmem_limit_bytes=60 * 2**20),
        cost_estimate=pl.CostEstimate(
            flops=2 * 2048 * 768 * 640, bytes_accessed=8 * 2**20, transcendentals=0
        ),
        name="project",
    )(coords, w_heads, *x_pairs)
    return outs[0:4], outs[4:8], outs[8], outs[9]


def unpack_kernel(coords, *refs):
    w_out, w_up, w_down = refs[4:7]
    for i, rest in enumerate(refs[0:4]):
        member = ((coords[2] + i % 2) % 2) * 2 + (coords[3] + i // 2) % 2
        rows = pl.ds(pl.multiple_of(member * 48, 16), 48)
        w_out[rows] = rest[0, 0:48]
        for i in range(4):
            w_up[rows, 768 * i : 768 * (i + 1)] = rest[0, 48 + 48 * i : 96 + 48 * i]
        w_down[pl.ds(pl.multiple_of(member * 192, 16), 192)] = rest[0, 240:432]


def unpacked(coords, *rests):
    block = pl.BlockSpec((1, 432, 768), lambda i: (i, 0, 0))
    return pl.pallas_call(
        unpack_kernel,
        grid=(4,),
        in_specs=[pl.BlockSpec(memory_space=pltpu.SMEM)] + [block] * 4,
        out_specs=[
            pl.BlockSpec((192, 768), lambda i: (i, 0)),
            pl.BlockSpec((192, 3072), lambda i: (i, 0)),
            pl.BlockSpec((768, 768), lambda i: (i, 0)),
        ],
        out_shape=[
            jax.ShapeDtypeStruct((768, 768), BF),
            jax.ShapeDtypeStruct((768, 3072), BF),
            jax.ShapeDtypeStruct((3072, 768), BF),
        ],
        compiler_params=pltpu.CompilerParams(vmem_limit_bytes=18 * 2**20),
        cost_estimate=pl.CostEstimate(flops=0, bytes_accessed=22 * 2**20, transcendentals=0),
        name="unpack_parameters",
    )(coords, *rests)


def collect(row, count, first, into):
    wide = row.shape[1]
    lanes = lax.broadcasted_iota(jnp.int32, (8, 768), 1)
    full = jnp.broadcast_to(row, (8, wide))
    inside = jnp.logical_and(lanes >= first, lanes < first + count)
    for s in range(16):
        shift = (first - s * count) % wide
        turned_row = pltpu.roll(full, shift, 1) if shift else full
        into[s] = jnp.where(inside, turned_row[:, :768], into[s])


def late_kernel(coords, *refs):
    narrow, wide, mine, send, back = refs[13], refs[14], refs[15], refs[16], refs[17:21]
    weights, x_all, near, far, sems, vec_scr = refs[21:27]
    y, first = coords[1], coords[3] == 0
    pairs = [(refs[0], weights)] + [(refs[1 + d], x_all.at[d]) for d in range(4)]
    pairs += [(refs[5 + d], near.at[d]) for d in range(4)]
    brought(pairs + [(refs[9 + d], far.at[d]) for d in range(4)], sems)
    ones = jnp.ones((256, 128), BF)
    totals, sums = [None] * 3, [None] * 3
    for c in range(8):
        back_part = jnp.zeros((768, 256), F32)
        for i in range(3):
            if c >= 4 and i == 0:
                continue
            grad = near[c, i] if c < 4 else far[c - 4, i - 1]
            grad = grad.reshape(192, 256)
            part = jnp.dot(grad, x_all[c % 4, c // 4], preferred_element_type=F32)
            row = jnp.dot(grad, ones, preferred_element_type=F32)
            totals[i] = part if totals[i] is None else totals[i] + part
            sums[i] = row if sums[i] is None else sums[i] + row
            back_part = back_part + jnp.dot(
                weights[:, 256 * i : 256 * i + 192], grad, preferred_element_type=F32
            )
        back[c % 4][c // 4] = back_part.T.astype(BF)
    gap = jnp.zeros((64, 768), F32)
    grads = jnp.concatenate([jnp.concatenate([t, gap], axis=0).T for t in totals], axis=1)
    for u in range(8):
        store_split(first, mine, send, u, 0, 48, grads[96 * u : 96 * u + 96])
    rows = []
    for i in (0, 2):
        row = jnp.concatenate([sums[i], jnp.zeros((64, 128), F32)], axis=0).T[0:8]
        rows.append(jnp.concatenate([row, jnp.zeros((8, 512), F32)], axis=1))
    lanes = lax.broadcasted_iota(jnp.int32, (8, 768), 1)
    vectors = []
    for j in range(4):
        query = pltpu.roll(rows[0], (768 - 48 * j) % 768, 1) if j else rows[0]
        shift = (768 + 48 - 48 * j) % 768
        value = pltpu.roll(rows[1], shift, 1) if shift else rows[1]
        vector = jnp.where(lanes < 48, query, jnp.where(lanes < 96, value, 0.0))
        vectors.append(vector)
    vec_scr[...] = jnp.zeros((16, 8, 768), F32)
    for i in range(6):
        collect(narrow[i : i + 1], 48, 48 * i, vec_scr)
    collect(wide[...], 192, 288, vec_scr)
    nothing = jnp.zeros((8, 768), F32)
    for u in range(8):
        both = [nothing, vec_scr[2 * u], nothing, vec_scr[2 * u + 1]]
        store_split(first, mine, send, u, 48, 16, jnp.concatenate(both, axis=0))
    for j in range(2):
        unit = 2 * y + j
        both = [vectors[2 * j], vec_scr[2 * unit], vectors[2 * j + 1], vec_scr[2 * unit + 1]]
        store_split(first, mine, send, unit, 48, 16, jnp.concatenate(both, axis=0))


def late_gradients(coords, w_heads, x_pairs, grad_msgs, narrow, wide):
    outs = pl.pallas_call(
        late_kernel,
        in_specs=[pl.BlockSpec(memory_space=pltpu.SMEM)]
        + [pl.BlockSpec(memory_space=pltpu.HBM)] * 13
        + [pl.BlockSpec(memory_space=pltpu.VMEM)] * 2,
        out_shape=[jax.ShapeDtypeStruct((8, 64, 768), BF)] * 2
        + [jax.ShapeDtypeStruct((2, 256, 768), BF)] * 4,
        scratch_shapes=[
            pltpu.VMEM((768, 896), BF),
            pltpu.VMEM((4, 2, 256, 768), BF),
            pltpu.VMEM((4, 3, GROUP, HD, 256), BF),
            pltpu.VMEM((4, 2, GROUP, HD, 256), BF),
            pltpu.SemaphoreType.DMA((17,)),
            pltpu.VMEM((16, 8, 768), F32),
        ],
        compiler_params=pltpu.CompilerParams(vmem_limit_bytes=60 * 2**20),
        cost_estimate=pl.CostEstimate(
            flops=4 * 2048 * 768 * 512, bytes_accessed=12 * 2**20, transcendentals=0
        ),
        name="late_gradients",
    )(coords, w_heads, *x_pairs, *grad_msgs, narrow, wide)
    return outs[0], outs[1], outs[2:]


def store_split(first, mine, send, unit, at, height, rows):
    even, odd = rows[:height], rows[height:]
    mine[unit, at : at + height] = jnp.where(first, even, odd).astype(BF)
    send[unit, at : at + height] = jnp.where(first, odd, even).astype(BF)


def down_kernel(coords, active_in, grad_in, mine, send, sems, active, grad_down):
    brought([(active_in, active), (grad_in, grad_down)], sems)
    first = coords[3] == 0
    for i in range(4):
        weights = lax.dot_general(
            active[:, 768 * i : 768 * (i + 1)],
            grad_down[...],
            (((0,), (0,)), ((), ())),
            preferred_element_type=F32,
        )
        for u in range(2):
            store_split(first, mine, send, 2 * i + u, 0, 192, weights[384 * u : 384 * u + 384])


def up_kernel(coords, *refs):
    mine, send, sems = refs[4:7]
    brought(list(zip(refs[0:4], refs[7:11])), sems)
    attended, hidden, grad_out, grad_up = refs[7:11]
    first = coords[3] == 0
    hidden_turned = hidden[...].astype(F32).T.astype(BF)
    for i in range(4):
        weights = jnp.dot(
            hidden_turned, grad_up[:, 768 * i : 768 * (i + 1)], preferred_element_type=F32
        )
        for u in range(8):
            store_split(first, mine, send, u, 48 + 48 * i, 48, weights[96 * u : 96 * u + 96])
    weights = jnp.dot(attended[...], grad_out[...], preferred_element_type=F32)
    for u in range(8):
        store_split(first, mine, send, u, 0, 48, weights[96 * u : 96 * u + 96])
    for u in range(8):
        mine[u, 240:256] = jnp.zeros((16, 768), BF)
        send[u, 240:256] = jnp.zeros((16, 768), BF)


def split_gradients(kernel, name, rows, blocks, scratch, coords, *arrays):
    return pl.pallas_call(
        kernel,
        in_specs=[pl.BlockSpec(memory_space=pltpu.SMEM)]
        + [pl.BlockSpec(memory_space=pl.ANY)] * len(arrays),
        out_shape=[jax.ShapeDtypeStruct((8, rows, 768), BF)] * 2,
        scratch_shapes=scratch,
        compiler_params=pltpu.CompilerParams(vmem_limit_bytes=20 * 2**20),
        cost_estimate=pl.CostEstimate(
            flops=2 * 256 * 768 * 768 * blocks, bytes_accessed=2 * 2**20 * blocks, transcendentals=0
        ),
        name=name,
    )(coords, *arrays)


def gelu_value(upward):
    return 0.5 * upward * (1.0 + lax.erf(upward * 0.7071067811865476))


def gelu_slope(upward):
    return (
        0.5 * (1.0 + lax.erf(upward * 0.7071067811865476))
        + upward * jnp.exp(-0.5 * upward * upward) * 0.3989422804014327
    )


def layer_norm(resid, gain, shift):
    mean = jnp.mean(resid, axis=-1, keepdims=True)
    centered = resid - mean
    spread = jnp.mean(centered * centered, axis=-1, keepdims=True)
    inverse = lax.rsqrt(spread + EPS)
    normed = centered * inverse
    return (normed * gain + shift, normed, inverse)


def norm_back(grad_out, normed, inverse, gain):
    grad_normed = grad_out * gain
    return inverse * (
        grad_normed
        - jnp.mean(grad_normed, axis=-1, keepdims=True)
        - normed * jnp.mean(grad_normed * normed, axis=-1, keepdims=True)
    )


def product(spec, left, right):
    return jnp.einsum(spec, left, right, preferred_element_type=F32)


def add(left, right):
    return (left.astype(F32) + right.astype(F32)).astype(BF)


def finish_sum(parts, z_hi):
    mine = add(pick(parts, z_hi), moved(pick(parts, 1 - z_hi), z_hi=1, z_lo=1))
    mine = add(mine, moved(mine, z_lo=1))
    return gathered(mine, 1)


def core_sum(mine, send):
    return add(mine, moved(send, core=1))


def along_x(units):
    return total(exchanged(units.reshape(4, 2, *units.shape[1:]), 0)).astype(BF)


def along_y(quarters, y):
    mine = pick(quarters, y).astype(F32)
    for d in (1, 3, 2):
        mine = mine + moved(pick(quarters, (y + d) % 4), y=d).astype(F32)
    return mine.astype(BF)


def finish_kernel(owned, w_qkv, w_out, w_up, w_down, vectors):
    rows = [owned[q].astype(F32) for q in range(4)]
    gap = jnp.zeros((48, 512), F32)
    for i in range(3):
        columns = jnp.zeros((48, 768), F32)
        for q in range(4):
            part = jnp.concatenate([rows[q][:48, 256 * i : 256 * (i + 1)], gap], axis=1)
            columns = columns + (pltpu.roll(part, 192 * q, 1) if q else part)
        w_qkv[:, 768 * i : 768 * (i + 1)] = columns
    early = jnp.concatenate([part[64:] for part in rows], axis=0)
    w_out[...] = early[0:48]
    for i in range(4):
        w_up[:, 768 * i : 768 * (i + 1)] = early[48 + 48 * i : 96 + 48 * i]
    w_down[...] = early[256:448]
    vectors[...] = rows[0][48:64] + rows[1][48:64] + rows[2][48:64] + rows[3][48:64]


def finished(owned):
    shapes = [(48, 2304), (48, 768), (48, 3072), (192, 768), (16, 768)]
    return pl.pallas_call(
        finish_kernel,
        out_shape=[jax.ShapeDtypeStruct(shape, F32) for shape in shapes],
        name="finish_gradients",
    )(owned)


def local(
    tokens,
    lengths,
    cotangent,
    w_qkv,
    b_query,
    b_value,
    w_out,
    b_out,
    gain_one,
    shift_one,
    w_up,
    b_up,
    w_down,
    b_down,
    gain_two,
    shift_two,
):
    ctx, shard = lax.axis_index("ctx"), lax.axis_index("shard")
    y, z_lo = ctx // 2, ctx % 2
    x, z_hi, core = shard // 4, (shard // 2) % 2, shard % 2
    width = 768
    x_low = tokens[0]

    x_pair = jnp.stack([x_low, moved(x_low, z_lo=1)])
    x_pairs = [x_pair] + [moved(x_pair, y=d) for d in (1, 2, 3)]

    coords = jnp.stack([x, y, z_hi, core]).astype(jnp.int32)
    vectors = jnp.stack([b_query, b_value, b_out, gain_one, shift_one, b_down, gain_two, shift_two])
    vectors = jnp.concatenate([vectors, b_up.reshape(4, 48)], axis=0)
    vectors = jnp.pad(vectors, [(0, 4), (0, 80)])
    heads_own, w_out = lax.optimization_barrier((packed(coords, w_qkv, vectors), w_out))
    w_heads = lax.all_gather(heads_own, "shard", axis=0, tiled=True)
    rest_own = joined(w_out, w_up, w_down)
    rest_other = moved(rest_own, z_hi=1, z_lo=1)
    rest = gathered(rest_own, 0)
    x_pairs[1], x_pairs[3], rest, rest_other = lax.optimization_barrier(
        (x_pairs[1], x_pairs[3], rest, rest_other)
    )
    rest_far = gathered(rest_other, 0)

    near, far, narrow, b_up = project(coords, w_heads, x_pairs)
    length = lengths[0]
    block_of = [((y - c) % 4) * 2 + (z_lo if c < 4 else 1 - z_lo) for c in range(8)]
    limits = jnp.stack([length - 256 * block for block in block_of]).astype(jnp.int32)
    *out_low, out_full, log_total = forward_attention(limits, near, far)
    _, rest_far = lax.optimization_barrier((out_low[0], rest_far))

    def in_order(parts):
        blocks = jnp.stack(parts + parts)
        return lax.dynamic_slice_in_dim(blocks, (4 - y) % 4, 4, 0)

    attended = in_order([out_low[0]] + [moved(out_low[d], y=4 - d) for d in (1, 2, 3)])
    attended = attended.reshape(width, 256)

    w_out, up_all, w_down = unpacked(
        coords, rest, rest_far, moved(rest, core=1), moved(rest_far, core=1)
    )
    b_out, gain_one, shift_one, b_down, gain_two, shift_two = (narrow[i] for i in range(6))
    resid_one = x_low.astype(F32) + product("kt,kd->td", attended, w_out) + b_out
    hidden, normed_one, inverse_one = layer_norm(resid_one, gain_one, shift_one)
    hidden_low = hidden.astype(BF)
    upward = product("td,df->tf", hidden_low, up_all) + b_up
    active_low = gelu_value(upward).astype(BF)
    resid_two = hidden + product("tf,fd->td", active_low, w_down) + b_down
    mixed, normed_two, inverse_two = layer_norm(resid_two, gain_two, shift_two)
    grad_mixed = cotangent[0].astype(F32)
    grad_gain_two = jnp.sum(grad_mixed * normed_two, axis=0)
    grad_shift_two = jnp.sum(grad_mixed, axis=0)
    grad_resid_two = norm_back(grad_mixed, normed_two, inverse_two, gain_two)
    grad_down_low = grad_resid_two.astype(BF)
    grad_b_down = jnp.sum(grad_resid_two, axis=0)
    down_split = split_gradients(
        down_kernel,
        "down_gradients",
        192,
        4,
        [pltpu.SemaphoreType.DMA((2,)), pltpu.VMEM((256, 3072), BF), pltpu.VMEM((256, 768), BF)],
        coords,
        active_low,
        grad_down_low,
    )
    down_units = core_sum(*down_split)
    grad_upward = product("td,fd->tf", grad_down_low, w_down) * gelu_slope(upward)
    grad_up_low = grad_upward.astype(BF)
    grad_b_up = jnp.sum(grad_upward, axis=0)
    grad_hidden = grad_resid_two + product("tf,df->td", grad_up_low, up_all)
    grad_gain_one = jnp.sum(grad_hidden * normed_one, axis=0)
    grad_shift_one = jnp.sum(grad_hidden, axis=0)
    grad_resid_one = norm_back(grad_hidden, normed_one, inverse_one, gain_one)
    grad_out_low = grad_resid_one.astype(BF)
    grad_b_out = jnp.sum(grad_resid_one, axis=0)
    grad_out_low, down_units = lax.optimization_barrier((grad_out_low, down_units))
    grad_attended = product("kd,td->kt", w_out, grad_out_low).astype(BF).reshape(4, GROUP, HD, 256)

    grads = [pick(grad_attended, y)]
    for d in (1, 2, 3):
        grads.append(moved(pick(grad_attended, (y + d) % 4), y=d))
    grad_narrow = jnp.stack(
        [grad_b_out, grad_gain_one, grad_shift_one, grad_b_down, grad_gain_two, grad_shift_two]
    )
    up_split = list(split_gradients(
        up_kernel,
        "up_gradients",
        256,
        5,
        [
            pltpu.SemaphoreType.DMA((4,)),
            pltpu.VMEM((768, 256), BF),
            pltpu.VMEM((256, 768), BF),
            pltpu.VMEM((256, 768), BF),
            pltpu.VMEM((256, 3072), BF),
        ],
        coords,
        attended,
        hidden_low,
        grad_out_low,
        grad_up_low,
    ))

    down_raw = exchanged(down_units.reshape(4, 2, 192, width), 0)
    up_units = core_sum(*up_split)
    grads, up_units = lax.optimization_barrier((grads, up_units))
    grad_msgs = list(backward_attention(limits, near, far, grads, out_full, log_total))
    up_units, down_raw, grad_msgs[0] = lax.optimization_barrier((up_units, down_raw, grad_msgs[0]))
    up_own = along_x(up_units)

    mine, send, back = late_gradients(
        coords, w_heads, x_pairs, grad_msgs, grad_narrow, grad_b_up[None]
    )
    late_units, up_own = lax.optimization_barrier((core_sum(mine, send), up_own))
    late = along_x(late_units)
    arrived = [moved(back[d], y=4 - d) for d in (1, 2, 3)]
    arrived[0], arrived[2], up_own = lax.optimization_barrier((arrived[0], arrived[2], up_own))
    grad_pair = back[0].astype(F32)
    for part in arrived:
        grad_pair = grad_pair + part.astype(F32)
    from_other = moved(grad_pair[1].astype(BF), z_lo=1)
    down_own = total(down_raw).astype(BF)
    early = jnp.concatenate([up_own, down_own], axis=1).reshape(2, 4, 112, width)
    early = along_y(early.transpose(1, 0, 2, 3), y)
    owned = finish_sum(jnp.concatenate([late, early], axis=1), z_hi)
    grad_w_qkv, grad_w_out, grad_w_up, grad_w_down, vectors = finished(owned)
    grad_tokens = grad_resid_one + grad_pair[0] + from_other.astype(F32)

    def early_vector(first, count=48):
        return vectors[8, first : first + count]

    return (
        mixed.astype(BF)[None],
        grad_tokens[None],
        grad_w_qkv,
        vectors[0, 0:48],
        vectors[0, 48:96],
        grad_w_out,
        early_vector(0),
        early_vector(48),
        early_vector(96),
        grad_w_up,
        early_vector(288, 192),
        grad_w_down,
        early_vector(144),
        early_vector(192),
        early_vector(240),
    )


def solution(mesh):
    rows, vector = P("shard", None), P("shard")
    tokens = P("shard", "ctx", None)
    return jax.shard_map(
        local,
        mesh=mesh,
        in_specs=(
            tokens, vector, tokens, rows, vector, vector, rows, vector, vector, vector,
            rows, vector, rows, vector, vector, vector,
        ),
        out_specs=(
            tokens, tokens, rows, vector, vector, rows, vector, vector, vector, rows,
            vector, rows, vector, vector, vector,
        ),
        check_vma=False,
    )
```
